256 devices in a mesh: slab: 16 (over z, core), cell: 16 (over x, y).
Axes of the slice: x: 4, y: 4, z: 8, core: 2. Of those that a mesh axis runs over, the one named last changes fastest.
Arguments:
- centers: float32 [3, 16384], P(None, ('slab', 'cell')), may hold values from -0.8 to 0.8
- offsets: float32 [3, 16384, 312], P(None, ('slab', 'cell')), may hold values from -0.5 to 0.5
- forces: float32 [3, 16384, 312], P(None, ('slab', 'cell')), may hold values from -6 to 6
- upsample: float32 [312, 1248], replicated, may hold values from -0.3125 to 0.3125
- translate: float32 [3, 165, 165], replicated, may hold values from -0.5 to 0.5
- owner_cell: int32 [256, 16, 2], P(('slab', 'cell')), may hold values from 0 to 63, as said below
- peer_cell: int32 [256, 16, 2], P(('slab', 'cell')), may hold values from 0 to 63, as said below
- live: int32 [256, 16, 2], P(('slab', 'cell')), may hold values 0 or 1
Outputs:
- velocity: float32 [3, 16384, 312], P(None, ('slab', 'cell'))
The draws below stay inside these ranges and needn't reach their ends.
Inputs may be any that keep to these rules, and one draw needn't show every extreme that they name: `owner_cell`: every cell takes part in at most one pair slot of all devices, as owner or as partner. `peer_cell`: every cell takes part in at most one pair slot of all devices, as owner or as partner.
All inputs are finite; a program needn't handle non-finite values. No bound on the sum of `live` on one device may be relied on, other than what follows from the above.
Results may differ from the reference program's by a relative error of at most 0.00019.
Values sent between devices are 32-bit elements; how exact they have to be, the bound alone decides.
A program may use at most 64 MiB of HBM per device.

```python
import math
import jax
import jax.numpy as jnp
from jax import lax

CELLS_DEV = 64
SLOT = 2
P_SIZE = 312
DEGREE = 8
UP = 1248
NT = 165
CELLS = 16384
N_SLAB = 16
N_CELL = 16


def place_value(order, value, position):
    where_now = jnp.argmax(order == value)
    held = order[position]
    return order.at[where_now].set(held).at[position].set(value)


def pair_lists(key):
    device_count = N_SLAB * N_CELL
    used = N_CELL * SLOT
    device_keys = jax.random.split(key, device_count)
    orders = jax.vmap(lambda one_key: jax.random.permutation(one_key, CELLS_DEV))(device_keys).astype(jnp.int32)
    first_row = place_value(place_value(orders[0], CELLS_DEV - 1, 0), 0, 1)
    second_row = place_value(place_value(orders[1], CELLS_DEV - 1, used), 0, used + 1)
    orders = orders.at[0].set(first_row).at[1].set(second_row)
    owners = orders[:, :used].reshape(device_count, N_CELL, SLOT)
    backward = orders[:, used:2 * used].reshape(N_SLAB, N_CELL, N_CELL, SLOT)
    partners = jnp.transpose(backward, (0, 2, 1, 3)).reshape(device_count, N_CELL, SLOT)
    return (owners, partners)


def draw_owner_cell(key, part):
    owners, partners = pair_lists(key)
    return owners


def draw_peer_cell(key, part):
    owners, partners = pair_lists(key)
    return partners


def draw_offsets(key, part):
    key = jax.random.fold_in(key, 11)
    radius_key, turn_key, rise_key, rough_key = jax.random.split(key, 4)
    radius = jax.random.uniform(radius_key, (CELLS,), jnp.float32, 0.22, 0.36)
    rough = jnp.clip(0.12 * jax.random.normal(rough_key, (CELLS, P_SIZE), jnp.float32), -0.3, 0.3)
    turn = jax.random.uniform(turn_key, (CELLS, P_SIZE), jnp.float32, -math.pi, math.pi)
    rise = jax.random.uniform(rise_key, (CELLS, P_SIZE), jnp.float32, -1.0, 1.0)
    flat = jnp.sqrt(jnp.maximum(1.0 - rise * rise, 0.0))
    direction = jnp.stack([flat * jnp.cos(turn), flat * jnp.sin(turn), rise])
    length = radius[:, None] * (1.0 + rough)
    return (length[None] * direction).astype(jnp.float32)


def draw_centers(key, part):
    owners, partners = pair_lists(key)
    key = jax.random.fold_in(key, 7)
    base_key, near_key, turn_key, rise_key = jax.random.split(key, 4)
    device_count = N_SLAB * N_CELL
    used = N_CELL * SLOT
    base = jax.random.uniform(base_key, (3, CELLS), jnp.float32, -0.6, 0.6)
    reach = jax.random.uniform(near_key, (device_count * used,), jnp.float32, 0.1, 0.2)
    turn = jax.random.uniform(turn_key, (device_count * used,), jnp.float32, -math.pi, math.pi)
    rise = jax.random.uniform(rise_key, (device_count * used,), jnp.float32, -1.0, 1.0)
    flat = jnp.sqrt(jnp.maximum(1.0 - rise * rise, 0.0))
    direction = jnp.stack([flat * jnp.cos(turn), flat * jnp.sin(turn), rise])
    device_ids = jnp.arange(device_count, dtype=jnp.int32)
    peer_ids = jnp.repeat(jnp.arange(N_CELL, dtype=jnp.int32), SLOT)
    first_cell = (device_ids[:, None] * CELLS_DEV + owners.reshape(device_count, used)).reshape(-1)
    second_cell = ((device_ids[:, None] // N_CELL * N_CELL + peer_ids[None, :]) * CELLS_DEV + partners.reshape(device_count, used)).reshape(-1)
    moved = base[:, first_cell] + reach[None, :] * direction
    return base.at[:, second_cell].set(moved).astype(jnp.float32)


def place_ends(result, rng, low, high):
    shape = result.shape
    place = [jax.random.randint(jax.random.fold_in(rng, axis), (), 0, shape[axis]) for axis in range(len(shape))]
    result = result.at[tuple(place)].set(low)
    longest = shape.index(max(shape))
    place[longest] = (place[longest] + 1) % shape[longest]
    return result.at[tuple(place)].set(high)


def levels(stream_key, extent, cuts, least, high):
    def one(axis_at, parts):
        heights = jax.random.uniform(jax.random.fold_in(jax.random.fold_in(stream_key, 6), axis_at), (parts,), jnp.float32, least / len(cuts), high / len(cuts))
        return jnp.repeat(jnp.exp(heights), extent[axis_at] // parts).reshape((-1,) + (1,) * (len(extent) - axis_at - 1))

    loudness = one(*cuts[0])
    for cut in cuts[1:]:
        loudness = loudness * one(*cut)
    return loudness


def scatter_about(stream_key, dims, width, most, cuts=(), kind=jnp.bfloat16):
    result = width * jax.random.normal(stream_key, dims, jnp.float32)
    if cuts:
        result = result * levels(stream_key, dims, cuts, -0.22, 0.18)
    return jnp.clip(result, -most, most).astype(kind)


def setup_inputs(seed: int = 0) -> dict:
    key_list = jax.random.split(jax.random.key(seed), 9)
    return {
        "centers": draw_centers(jax.random.fold_in(key_list[8], 71), 0),
        "offsets": draw_offsets(jax.random.fold_in(key_list[8], 71), 0),
        "forces": scatter_about(key_list[2], (3, CELLS, P_SIZE), 1.0, 6.0, ((1, 256),), jnp.float32),
        "upsample": scatter_about(key_list[3], (P_SIZE, UP), P_SIZE ** -0.5, 0.3125, (), jnp.float32),
        "translate": scatter_about(key_list[4], (3, NT, NT), NT ** -0.5, 0.5, (), jnp.float32),
        "owner_cell": draw_owner_cell(jax.random.fold_in(key_list[8], 71), 0),
        "peer_cell": draw_peer_cell(jax.random.fold_in(key_list[8], 71), 0),
        "live": place_ends((jax.random.randint(key_list[7], (N_SLAB * N_CELL, N_CELL, SLOT), 0, 2) < 1).astype(jnp.int32), jax.random.fold_in(key_list[7], 1), 0, 1),
    }


soften = 0.0025
highest = lax.Precision.HIGHEST

def stokeslet(targets, sources, strengths):
    differ = targets[:, :, None] - sources[:, None, :]
    radius_sq = lax.optimization_barrier(jnp.sum(differ * differ, axis=0))
    inverse = lax.rsqrt(radius_sq + soften)
    inverse_cube = inverse * inverse * inverse
    projected = lax.optimization_barrier(jnp.sum(differ * strengths[:, None, :], axis=0))
    summed = (radius_sq + 2.0 * soften)[None] * strengths[:, None, :] + projected[None] * differ
    return lax.optimization_barrier(jnp.sum(summed * inverse_cube[None], axis=2)) / sources.shape[1]

def monomials(points):
    powers_x = [jnp.ones_like(points[0])]
    powers_y = [jnp.ones_like(points[1])]
    powers_z = [jnp.ones_like(points[2])]
    for number in range(DEGREE):
        powers_x.append(powers_x[-1] * points[0])
        powers_y.append(powers_y[-1] * points[1])
        powers_z.append(powers_z[-1] * points[2])
    terms = []
    for first in range(DEGREE + 1):
        for second in range(DEGREE + 1 - first):
            for third in range(DEGREE + 1 - first - second):
                terms.append(powers_x[first] * powers_y[second] * powers_z[third])
    return jnp.stack(terms)

def reference(centers, offsets, forces, upsample, translate, owner_cell, peer_cell, live):
    cells_all = centers.shape[1]
    device_count = N_SLAB * N_CELL
    per_device = N_CELL * SLOT
    points = centers[:, :, None] + offsets
    device_ids = jnp.arange(device_count, dtype=jnp.int32)
    peer_ids = jnp.repeat(jnp.arange(N_CELL, dtype=jnp.int32), SLOT)
    first_cell = device_ids[:, None] * CELLS_DEV + owner_cell.reshape(device_count, per_device)
    second_cell = (device_ids[:, None] // N_CELL * N_CELL + peer_ids[None, :]) * CELLS_DEV + peer_cell.reshape(device_count, per_device)
    live_weight = live.reshape(device_count, per_device).astype(jnp.float32)

    def upsampled(cell_index):
        spread = centers[:, cell_index][:, None] + jnp.dot(offsets[:, cell_index], upsample, precision=highest)
        strength = jnp.dot(forces[:, cell_index], upsample, precision=highest)
        return (spread, strength)

    def one_pair(cell_a, cell_b, weight):
        spread_a, strength_a = upsampled(cell_a)
        spread_b, strength_b = upsampled(cell_b)
        on_b = stokeslet(points[:, cell_b], spread_a, strength_a) * weight
        on_a = stokeslet(points[:, cell_a], spread_b, strength_b) * weight
        return (on_a, on_b)

    def one_device(operands):
        return jax.vmap(one_pair)(operands[0], operands[1], operands[2])
    on_a, on_b = lax.map(one_device, (first_cell, second_cell, live_weight))
    near_field = jnp.zeros((3, cells_all, P_SIZE), jnp.float32)
    near_field = near_field.at[:, first_cell.reshape(-1)].add(jnp.moveaxis(on_a.reshape(-1, 3, P_SIZE), 0, 1))
    near_field = near_field.at[:, second_cell.reshape(-1)].add(jnp.moveaxis(on_b.reshape(-1, 3, P_SIZE), 0, 1))
    moment_scale = 1.0 / math.sqrt(N_CELL * CELLS_DEV * P_SIZE)
    slab_points = jnp.moveaxis(points.reshape(3, N_SLAB, N_CELL * CELLS_DEV * P_SIZE), 1, 0)
    slab_forces = jnp.moveaxis(forces.reshape(3, N_SLAB, N_CELL * CELLS_DEV * P_SIZE), 1, 0)

    def moment(operands):
        return jnp.dot(monomials(operands[0]), operands[1].T, precision=highest) * moment_scale
    moments = lax.map(moment, (slab_points, slab_forces))
    empty_slab = jnp.zeros((1, NT, 3), jnp.float32)
    from_below = jnp.concatenate([empty_slab, moments[:-1]], axis=0)
    from_above = jnp.concatenate([moments[1:], empty_slab], axis=0)
    local_coef = jnp.einsum('kj,sjc->skc', translate[0], moments, precision=highest)
    local_coef = local_coef + jnp.einsum('kj,sjc->skc', translate[1], from_below, precision=highest)
    local_coef = local_coef + jnp.einsum('kj,sjc->skc', translate[2], from_above, precision=highest)

    def evaluate(operands):
        return jnp.dot(operands[1].T, monomials(operands[0]), precision=highest)
    far_field = lax.map(evaluate, (slab_points, local_coef))
    far_field = jnp.moveaxis(far_field, 0, 1).reshape(3, cells_all, P_SIZE)
    return near_field + far_field
```

```python
import functools
import math

import jax
import jax.numpy as jnp
from jax import lax
from jax.experimental import pallas as pl
from jax.experimental.pallas import tpu as pltpu
from jax.sharding import PartitionSpec as P

DEGREE = 8
NT = 165
SOFTEN = 0.0025
STRETCH = 20.0
LANES = 384
UP_LANES = 1280
f32 = jnp.float32
bf16 = jnp.bfloat16
MESH = pl.DeviceIdType.MESH
highest = lax.Precision.HIGHEST
NT_DIMS = (((1,), (1,)), ((), ()))


def split3(x):
    first = x.astype(bf16).astype(f32)
    rest = x - first
    second = rest.astype(bf16).astype(f32)
    third = (rest - second).astype(bf16).astype(f32)
    return first, second, third


def exchange_kernel(
    owner, peer, live, centers, offsets, forces, translate,
    got_a, got_b, got_meta, block, points, local,
    send_a, send_b, send_meta, meta_here, mom_out, mom_in, total, beside, padded, acc,
    send_sems, recv_sems, side_send, side_recv, here_sem,
):
    n_cell = lax.axis_size("cell")
    n_slab = lax.axis_size("slab")
    me = lax.axis_index("cell")
    slab = lax.axis_index("slab")
    above = lax.rem(slab + 1, n_slab)
    below = lax.rem(slab + n_slab - 1, n_slab)
    cells, count = offsets.shape[1], offsets.shape[2]

    barrier = pltpu.get_barrier_semaphore()

    def greet(j, carry):
        to = lax.rem(me + j, n_cell)
        pl.semaphore_signal(barrier, inc=1, device_id={"cell": to}, device_id_type=MESH)
        return carry

    lax.fori_loop(1, n_cell, greet, 0)
    for side in (above, below):
        pl.semaphore_signal(barrier, inc=1, device_id={"slab": side}, device_id_type=MESH)

    lane = lax.broadcasted_iota(jnp.int32, (cells, LANES), 1)
    diag = lax.broadcasted_iota(jnp.int32, (cells, cells), 0) == lax.broadcasted_iota(jnp.int32, (cells, cells), 1)
    block[...] = jnp.zeros_like(block)
    for d in range(3):
        column = jnp.sum(jnp.where(diag, centers[d : d + 1, :], 0.0), axis=1, keepdims=True)
        padded[d, :, 0:count] = offsets[d]
        padded[3 + d, :, 0:count] = forces[d]
        shift = jnp.where(lane < count, padded[d], jnp.where(lane == count, column, 0.0))
        force = jnp.where(lane < count, padded[3 + d], 0.0)
        block[:, d, :] = shift
        block[:, 4 + d, :] = force
        padded[3 + d] = force
        points[d] = jnp.where(lane < count, shift + column, 0.0)

    small = lax.broadcasted_iota(jnp.int32, (8, 128), 1)
    for q in range(n_cell):
        for k in range(2):
            send_a[q, k] = block[owner[0, q, k]]
        row = jnp.where(small == 0, peer[0, q, 0], peer[0, q, 1])
        row = jnp.where(small == 2, live[0, q, 0], row)
        send_meta[q] = jnp.where(small == 3, live[0, q, 1], row)

    pl.semaphore_wait(barrier, n_cell + 1)

    def copy(kind, source, target, j):
        to = lax.rem(me + j, n_cell)
        return pltpu.make_async_remote_copy(
            src_ref=source if kind == 3 else source.at[to],
            dst_ref=target.at[me],
            send_sem=send_sems.at[kind, j],
            recv_sem=recv_sems.at[kind, j],
            device_id={"cell": to},
            device_id_type=MESH,
        )

    def each(action):
        def step(j, carry):
            action(j)
            return carry

        lax.fori_loop(1, n_cell, step, 0)

    def arrival(kind, source, target, j):
        origin = lax.rem(me + n_cell - j, n_cell)
        return pltpu.make_async_remote_copy(
            src_ref=source if kind == 3 else source.at[origin],
            dst_ref=target.at[origin],
            send_sem=send_sems.at[kind, j],
            recv_sem=recv_sems.at[kind, j],
            device_id={"cell": origin},
            device_id_type=MESH,
        )

    each(lambda j: copy(0, send_meta, got_meta, j).start())
    each(lambda j: copy(1, send_a, got_a, j).start())
    got_meta[me] = send_meta[me]
    got_a[me] = send_a[me]
    each(lambda j: arrival(0, send_meta, got_meta, j).wait_recv())
    fetch = pltpu.make_async_copy(got_meta, meta_here, here_sem)
    fetch.start()
    fetch.wait()
    for q in range(n_cell):
        for k in range(2):
            send_b[q, k] = block[meta_here[q, 0, k]]
    each(lambda j: copy(2, send_b, got_b, j).start())
    got_b[me] = send_b[me]

    acc[...] = jnp.zeros_like(acc)

    def moment_rows(i, carry):
        rows = pl.ds(pl.multiple_of(i * 8, 8), 8)
        x, y, z = points[0, rows], points[1, rows], points[2, rows]
        force = [padded[3 + d, rows] for d in range(3)]
        t = 0
        power_x = jnp.ones_like(x)
        for a in range(DEGREE + 1):
            power_y = power_x
            for b in range(DEGREE + 1 - a):
                term = power_y
                for c in range(DEGREE + 1 - a - b):
                    for d in range(3):
                        v = term * force[d]
                        acc[d, t] += v[:, 0:128] + v[:, 128:256] + v[:, 256:384]
                    t += 1
                    if c < DEGREE - a - b:
                        term = term * z
                if b < DEGREE - a:
                    power_y = power_y * y
            if a < DEGREE:
                power_x = power_x * x
        return carry

    lax.fori_loop(0, cells // 8, moment_rows, 0)
    scale = 1.0 / math.sqrt(cells * n_cell * count)
    terms = acc.shape[1]
    sub = lax.broadcasted_iota(jnp.int32, (8, terms), 0)
    moments = jnp.zeros((8, terms), f32)
    for d in range(3):
        part = jnp.sum(acc[d], axis=1)
        row = lax.dot_general(jnp.ones((8, 128), f32), part, NT_DIMS, precision=highest, preferred_element_type=f32)
        moments = jnp.where(sub == d, row * scale, moments)
    mom_out[...] = jnp.zeros_like(mom_out)
    mom_out[:, 0:terms] = moments
    each(lambda j: copy(3, mom_out, mom_in, j).start())
    mom_in[me] = mom_out[...]
    each(lambda j: arrival(3, mom_out, mom_in, j).wait_recv())
    gathered = mom_in[0]
    for q in range(1, n_cell):
        gathered = gathered + mom_in[q]
    total[...] = gathered

    def side_copy(which, to):
        return pltpu.make_async_remote_copy(
            src_ref=total,
            dst_ref=beside.at[which],
            send_sem=side_send.at[which],
            recv_sem=side_recv.at[which],
            device_id={"slab": to},
            device_id_type=MESH,
        )

    up_copy, down_copy = side_copy(0, above), side_copy(1, below)
    up_copy.start()
    down_copy.start()
    up_copy.wait()
    down_copy.wait()
    lower = jnp.where(slab == 0, 0.0, beside[0])
    upper = jnp.where(slab == n_slab - 1, 0.0, beside[1])
    coef = jnp.zeros((8, NT), f32)
    for k, source in enumerate((total[...], lower, upper)):
        coef = coef + lax.dot_general(
            source[:, 0:NT], translate[k], NT_DIMS, precision=highest, preferred_element_type=f32
        )
    local[...] = jnp.zeros_like(local)
    local[:, 0:NT] = coef

    each(lambda j: arrival(1, send_a, got_a, j).wait_recv())
    each(lambda j: arrival(2, send_b, got_b, j).wait_recv())
    each(lambda j: copy(0, send_meta, got_meta, j).wait_send())
    each(lambda j: copy(1, send_a, got_a, j).wait_send())
    each(lambda j: copy(2, send_b, got_b, j).wait_send())
    each(lambda j: copy(3, mom_out, mom_in, j).wait_send())


def field_kernel(
    meta, owner, live, local, block, got_a, got_b, points, upsample,
    out,
    cell_list, packed, spread, up_high, up_low, left, right, table, columns,
):
    cells, count, up_count = out.shape[1], out.shape[2], upsample.shape[1]
    n_cell = got_a.shape[0]

    def far_rows(i, carry):
        rows = pl.ds(pl.multiple_of(i * 16, 16), 16)
        x, y, z = points[0, rows], points[1, rows], points[2, rows]
        index = {}
        t = 0
        for a in range(DEGREE + 1):
            for b in range(DEGREE + 1 - a):
                for c in range(DEGREE + 1 - a - b):
                    index[a, b, c] = t
                    t += 1
        for d in range(3):
            in_x = None
            for a in range(DEGREE, -1, -1):
                in_y = None
                for b in range(DEGREE - a, -1, -1):
                    in_z = None
                    for c in range(DEGREE - a - b, -1, -1):
                        value = local[d, index[a, b, c]]
                        in_z = value if in_z is None else in_z * z + value
                    in_y = in_z if in_y is None else in_y * y + in_z
                in_x = in_y if in_x is None else in_x * x + in_y
            out[d, rows, :] = in_x[:, 0:count]
        return carry

    lax.fori_loop(0, cells // 16, far_rows, 0)

    def list_slot(s, n):
        q, k = s // 2, lax.rem(s, 2)
        flag, cell = live[0, q, k], owner[0, q, k]

        @pl.when(flag > 0)
        def _():
            cell_list[n] = cell
            packed[n] = got_b[q, k]

        n = n + jnp.where(flag > 0, 1, 0)
        flag_in, cell_in = meta[q, 0, 2 + k], meta[q, 0, k]

        @pl.when(flag_in > 0)
        def _():
            cell_list[n] = cell_in
            packed[n] = got_a[q, k]

        return n + jnp.where(flag_in > 0, 1, 0)

    units = lax.fori_loop(0, 2 * n_cell, list_slot, jnp.int32(0))

    up_high[...] = jnp.zeros_like(up_high)
    up_low[...] = jnp.zeros_like(up_low)
    whole = upsample[...]
    high = whole.astype(bf16)
    up_high[:, 0:up_count] = high
    up_low[:, 0:up_count] = (whole - high.astype(f32)).astype(bf16)

    def spread_units(i, carry):
        rows = pl.ds(i * 16, 16)
        data = packed[rows].reshape(128, LANES)[:, 0:count]
        first = data.astype(bf16)
        second = (data - first.astype(f32)).astype(bf16)
        result = (
            jnp.dot(first, up_high[...], preferred_element_type=f32)
            + jnp.dot(second, up_high[...], preferred_element_type=f32)
            + jnp.dot(first, up_low[...], preferred_element_type=f32)
        )
        spread[rows] = result.reshape(16, 8, UP_LANES)
        return carry

    lax.fori_loop(0, (units + 15) // 16, spread_units, 0)

    def build(u, carry):
        cell = cell_list[u]
        target = block[cell]
        row = lax.broadcasted_iota(jnp.int32, (8, UP_LANES), 0)
        between = packed[u][:, count : count + 1] - target[:, count : count + 1]
        z = jnp.where(row < 3, STRETCH * (spread[u] + between), spread[u])
        table[u] = z
        square = jnp.sum(jnp.where(row < 3, z * z, 0.0), axis=0, keepdims=True) + 1.0
        aligned = jnp.concatenate([z[4:8], z[0:4]], axis=0)
        product = jnp.sum(jnp.where(row < 3, z * aligned, 0.0), axis=0, keepdims=True)
        feature = jnp.where(row < 3, -2.0 * z, jnp.where(row == 3, square, jnp.where(row == 7, -product, z)))
        f1, f2, f3 = split3(feature)
        constant = jnp.where(row < 3, 1.0, 0.0)
        for k, pair in enumerate(((f1, f2), (f1, f3), (f2, f1), (constant, jnp.zeros_like(constant)))):
            right[u, 16 * k : 16 * k + 16] = jnp.concatenate(pair, axis=0).astype(bf16)

        small = lax.broadcasted_iota(jnp.int32, (8, LANES), 0)
        y = jnp.where(small < 3, STRETCH * target, 0.0)
        yy = jnp.sum(y * y, axis=0, keepdims=True)
        y1, y2, y3 = split3(y)
        s1, s2, s3 = split3(yy)
        one = jnp.where(small == 3, 1.0, y1)
        squares = jnp.where(small == 0, s1, jnp.where(small == 1, s2, jnp.where(small == 2, s3, 0.0)))
        zero = jnp.zeros_like(y)
        order = [one, one, y2, one, y2, y3]
        lower = [jnp.concatenate([v[4:8], v[0:4]], axis=0) for v in order]
        for k, rows in enumerate((order + [squares, zero], lower + [zero, zero])):
            turned = jnp.transpose(jnp.concatenate(rows, axis=0))
            left[u, k] = turned[0:count].astype(bf16)
        return carry

    lax.fori_loop(0, units, build, 0)

    columns[...] = jnp.zeros_like(columns)
    step = 40

    def one_unit(u, carry):
        cell = cell_list[u]
        for begin in range(0, count, step):
            size = min(step, count - begin)
            near = [jnp.zeros((size, 128), f32) for _ in range(4)]
            left_s = left[u, 0, begin : begin + size]
            left_p = left[u, 1, begin : begin + size]
            for c in range(UP_LANES // 128):
                lanes = slice(c * 128, c * 128 + 128)
                feature = right[u, :, lanes]
                inverse = lax.rsqrt(jnp.dot(left_s, feature, preferred_element_type=f32))
                projected = jnp.dot(left_p, feature, preferred_element_type=f32)
                cube = inverse * inverse * inverse
                along = inverse + cube
                across = cube * projected
                for d in range(3):
                    near[d] = near[d] + (
                        along * table[u, 4 + d : 5 + d, lanes] - across * table[u, d : d + 1, lanes]
                    )
                near[3] = near[3] + across
            for d in range(4):
                columns[begin : begin + size, d : d + 1] = jnp.sum(near[d], axis=1, keepdims=True)
        sums = jnp.transpose(columns[...])[0:8]
        small = lax.broadcasted_iota(jnp.int32, (8, LANES), 0)
        y = jnp.where(small < 3, STRETCH * block[cell], 0.0)
        velocity = (sums + y * sums[3:4]) * (STRETCH / up_count)
        for d in range(3):
            out[d, pl.ds(cell, 1), :] += velocity[d : d + 1, 0:count]
        return carry

    lax.fori_loop(0, units, one_unit, 0)


def on_device(centers, offsets, forces, upsample, translate, owner_cell, peer_cell, live):
    cells, count = offsets.shape[1], offsets.shape[2]
    n_cell = owner_cell.shape[1]
    vmem = pl.BlockSpec(memory_space=pltpu.VMEM)
    smem = pl.BlockSpec(memory_space=pltpu.SMEM)
    slots = (n_cell, 2, 8, LANES)
    got_a, got_b, got_meta, block, points, local = pl.pallas_call(
        exchange_kernel,
        out_shape=(
            jax.ShapeDtypeStruct(slots, f32),
            jax.ShapeDtypeStruct(slots, f32),
            jax.ShapeDtypeStruct((n_cell, 8, 128), jnp.int32),
            jax.ShapeDtypeStruct((cells, 8, LANES), f32),
            jax.ShapeDtypeStruct((3, cells, LANES), f32),
            jax.ShapeDtypeStruct((8, 256), f32),
        ),
        in_specs=[smem] * 3 + [vmem] * 4,
        out_specs=(vmem,) * 6,
        scratch_shapes=[
            pltpu.VMEM(slots, f32),
            pltpu.VMEM(slots, f32),
            pltpu.VMEM((n_cell, 8, 128), jnp.int32),
            pltpu.SMEM((n_cell, 8, 128), jnp.int32),
            pltpu.VMEM((8, 256), f32),
            pltpu.VMEM((n_cell, 8, 256), f32),
            pltpu.VMEM((8, 256), f32),
            pltpu.VMEM((2, 8, 256), f32),
            pltpu.VMEM((6, cells, LANES), f32),
            pltpu.VMEM((3, 168, 8, 128), f32),
            pltpu.SemaphoreType.DMA((4, n_cell)),
            pltpu.SemaphoreType.DMA((4, n_cell)),
            pltpu.SemaphoreType.DMA((2,)),
            pltpu.SemaphoreType.DMA((2,)),
            pltpu.SemaphoreType.DMA,
        ],
        compiler_params=pltpu.CompilerParams(
            collective_id=0, has_side_effects=True, vmem_limit_bytes=32 * 1024 * 1024
        ),
        name="exchange",
    )(owner_cell, peer_cell, live, centers, offsets, forces, translate)
    return pl.pallas_call(
        field_kernel,
        out_shape=jax.ShapeDtypeStruct((3, cells, count), f32),
        in_specs=[smem] * 4 + [vmem] * 5,
        out_specs=vmem,
        scratch_shapes=[
            pltpu.SMEM((cells,), jnp.int32),
            pltpu.VMEM((cells, 8, LANES), f32),
            pltpu.VMEM((cells, 8, UP_LANES), f32),
            pltpu.VMEM((count, UP_LANES), bf16),
            pltpu.VMEM((count, UP_LANES), bf16),
            pltpu.VMEM((cells, 2, count, 64), bf16),
            pltpu.VMEM((cells, 64, UP_LANES), bf16),
            pltpu.VMEM((cells, 8, UP_LANES), f32),
            pltpu.VMEM((LANES, 128), f32),
        ],
        compiler_params=pltpu.CompilerParams(vmem_limit_bytes=50 * 1024 * 1024),
        name="field",
    )(got_meta, owner_cell, live, local, block, got_a, got_b, points, upsample)


def solution(mesh):
    return jax.shard_map(
        on_device,
        mesh=mesh,
        in_specs=(
            P(None, ("slab", "cell")),
            P(None, ("slab", "cell"), None),
            P(None, ("slab", "cell"), None),
            P(),
            P(),
            P(("slab", "cell"), None, None),
            P(("slab", "cell"), None, None),
            P(("slab", "cell"), None, None),
        ),
        out_specs=P(None, ("slab", "cell"), None),
        check_vma=False,
    )
```

```python
import functools
import math

import jax
import jax.numpy as jnp
from jax import lax
from jax.experimental import pallas as pl
from jax.experimental.pallas import tpu as pltpu
from jax.sharding import PartitionSpec as P

DEGREE = 8
NT = 165
SOFTEN = 0.0025
STRETCH = 20.0
LANES = 384
UP_LANES = 1280
f32 = jnp.float32
bf16 = jnp.bfloat16
MESH = pl.DeviceIdType.MESH
highest = lax.Precision.HIGHEST
NT_DIMS = (((1,), (1,)), ((), ()))


def split3(x):
    first = x.astype(bf16).astype(f32)
    rest = x - first
    second = rest.astype(bf16).astype(f32)
    third = (rest - second).astype(bf16).astype(f32)
    return first, second, third


def exchange_kernel(
    owner, peer, live, centers_hbm, offsets_hbm, forces_hbm, translate_hbm,
    got_a, got_b, meta, block, points, local,
    centers, offsets, forces, translate, sent, send_a, send_b, send_meta, got_meta, merged, meta_here,
    mom_out, mom_in, total, beside, padded, acc,
    send_sems, recv_sems, side_send, side_recv, here_sems,
):
    n_cell = lax.axis_size("cell")
    n_slab = lax.axis_size("slab")
    me = lax.axis_index("cell")
    slab = lax.axis_index("slab")
    above = lax.rem(slab + 1, n_slab)
    below = lax.rem(slab + n_slab - 1, n_slab)
    cells, count = offsets.shape[1], offsets.shape[2]

    barrier = pltpu.get_barrier_semaphore()
    pairs = ((centers_hbm, centers), (offsets_hbm, offsets), (forces_hbm, forces), (translate_hbm, translate))
    loads = [pltpu.make_async_copy(source, target, here_sems.at[k]) for k, (source, target) in enumerate(pairs)]
    for load in loads:
        load.start()

    def greet(j, carry):
        to = lax.rem(me + j, n_cell)
        pl.semaphore_signal(barrier, inc=1, device_id={"cell": to}, device_id_type=MESH)
        return carry

    lax.fori_loop(1, n_cell, greet, 0)
    for side in (above, below):
        pl.semaphore_signal(barrier, inc=1, device_id={"slab": side}, device_id_type=MESH)

    small = lax.broadcasted_iota(jnp.int32, (8, 128), 1) - 4 * me
    for q in range(n_cell):
        row = jnp.zeros((8, 128), jnp.int32)
        for k in range(2):
            row = jnp.where(small == k, peer[0, k, q], row)
            row = jnp.where(small == 2 + k, live[0, k, q], row)
        send_meta[q] = row

    for load in loads[:3]:
        load.wait()

    lane = lax.broadcasted_iota(jnp.int32, (cells, LANES), 1)
    tail_lane = lax.broadcasted_iota(jnp.int32, (cells, 128), 1)
    diag = lax.broadcasted_iota(jnp.int32, (cells, cells), 0) == lax.broadcasted_iota(jnp.int32, (cells, cells), 1)
    block[...] = jnp.zeros_like(block)
    tails = []
    middle = jnp.zeros((cells, 128), f32)
    for d in range(3):
        column = jnp.sum(jnp.where(diag, centers[d : d + 1, :], 0.0), axis=1, keepdims=True)
        padded[d, :, 0:count] = offsets[d]
        padded[3 + d, :, 0:count] = forces[d]
        offset = jnp.where(lane < count, padded[d], 0.0)
        force = jnp.where(lane < count, padded[3 + d], 0.0)
        block[:, d, :] = jnp.where(lane == count, column, offset)
        block[:, 4 + d, :] = force
        sent[:, d, :] = offset[:, 0:256]
        sent[:, 4 + d, :] = force[:, 0:256]
        padded[3 + d] = force
        points[d] = jnp.where(lane < count, offset + column, 0.0)
        tails.append((offset[:, 256:384], force[:, 256:384]))
        middle = jnp.where(tail_lane == 64 + d, column, middle)
    for k in range(2):
        sent[:, 3 + 4 * k, 0:128] = tails[0][k] + pltpu.roll(tails[1][k], 64, 1)
        sent[:, 3 + 4 * k, 128:256] = tails[2][k] + middle

    for q in range(n_cell):
        for k in range(2):
            send_a[q, k] = sent[owner[0, k, q]]

    pl.semaphore_wait(barrier, n_cell + 1)

    def send(kind, source, target):
        def step(j, carry):
            to = lax.rem(me + j, n_cell)
            pltpu.make_async_remote_copy(
                src_ref=source if kind == 3 else source.at[to],
                dst_ref=target.at[me],
                send_sem=send_sems.at[kind],
                recv_sem=recv_sems.at[kind],
                device_id={"cell": to},
                device_id_type=MESH,
            ).start()
            return carry

        lax.fori_loop(1, n_cell, step, 0)

    def every(kind, target):
        part = target.at[pl.ds(0, n_cell - 1)]
        return pltpu.make_async_remote_copy(
            src_ref=part,
            dst_ref=part,
            send_sem=send_sems.at[kind],
            recv_sem=recv_sems.at[kind],
            device_id={"cell": lax.rem(me + 1, n_cell)},
            device_id_type=MESH,
        )

    send(0, send_meta, got_meta)
    send(1, send_a, got_a)
    got_meta[me] = send_meta[me]
    got_a[me] = send_a[me]
    every(0, got_meta).wait_recv()
    whole = got_meta[0]
    for q in range(1, n_cell):
        whole = whole + got_meta[q]
    merged[...] = whole[0:1]
    meta[...] = whole[0:1]
    fetch = pltpu.make_async_copy(merged, meta_here, here_sems.at[0])
    fetch.start()
    fetch.wait()
    for q in range(n_cell):
        for k in range(2):
            send_b[q, k] = sent[meta_here[0, 4 * q + k]]
    send(2, send_b, got_b)
    got_b[me] = send_b[me]

    acc[...] = jnp.zeros_like(acc)

    def moment_rows(i, carry):
        rows = pl.ds(pl.multiple_of(i * 8, 8), 8)
        x, y, z = points[0, rows], points[1, rows], points[2, rows]
        force = [padded[3 + d, rows] for d in range(3)]
        t = 0
        power_x = jnp.ones_like(x)
        for a in range(DEGREE + 1):
            power_y = power_x
            for b in range(DEGREE + 1 - a):
                term = power_y
                for c in range(DEGREE + 1 - a - b):
                    for d in range(3):
                        v = term * force[d]
                        acc[d, t] += v[:, 0:128] + v[:, 128:256] + v[:, 256:384]
                    t += 1
                    if c < DEGREE - a - b:
                        term = term * z
                if b < DEGREE - a:
                    power_y = power_y * y
            if a < DEGREE:
                power_x = power_x * x
        return carry

    lax.fori_loop(0, cells // 8, moment_rows, 0)
    scale = 1.0 / math.sqrt(cells * n_cell * count)
    terms = acc.shape[1]
    sub = lax.broadcasted_iota(jnp.int32, (8, terms), 0)
    moments = jnp.zeros((8, terms), f32)
    for d in range(3):
        part = jnp.sum(acc[d], axis=1)
        row = lax.dot_general(jnp.ones((8, 128), f32), part, NT_DIMS, precision=highest, preferred_element_type=f32)
        moments = jnp.where(sub == d, row * scale, moments)
    mom_out[...] = jnp.zeros_like(mom_out)
    mom_out[:, 0:terms] = moments
    send(3, mom_out, mom_in)
    mom_in[me] = mom_out[...]
    every(3, mom_in).wait_recv()
    gathered = mom_in[0]
    for q in range(1, n_cell):
        gathered = gathered + mom_in[q]
    total[...] = gathered

    def side_copy(which, to):
        return pltpu.make_async_remote_copy(
            src_ref=total,
            dst_ref=beside.at[which],
            send_sem=side_send.at[which],
            recv_sem=side_recv.at[which],
            device_id={"slab": to},
            device_id_type=MESH,
        )

    up_copy, down_copy = side_copy(0, above), side_copy(1, below)
    up_copy.start()
    down_copy.start()
    up_copy.wait()
    down_copy.wait()
    lower = jnp.where(slab == 0, 0.0, beside[0])
    upper = jnp.where(slab == n_slab - 1, 0.0, beside[1])
    coef = jnp.zeros((8, NT), f32)
    loads[3].wait()
    for k, source in enumerate((total[...], lower, upper)):
        coef = coef + lax.dot_general(
            source[:, 0:NT], translate[k], NT_DIMS, precision=highest, preferred_element_type=f32
        )
    local[...] = coef[0:3]

    every(1, got_a).wait_recv()
    every(2, got_b).wait_recv()
    every(0, got_meta).wait_send()
    every(1, got_a).wait_send()
    every(2, got_b).wait_send()
    every(3, mom_in).wait_send()


def field_kernel(
    meta, owner, live, local, block, got_a, got_b, points, upsample_hbm,
    out,
    cell_list, upsample, packed, spread, up_high, up_low, left, right, table, columns, load_sem,
):
    load = pltpu.make_async_copy(upsample_hbm, upsample, load_sem)
    load.start()
    cells, count, up_count = out.shape[1], out.shape[2], upsample.shape[1]
    n_cell = got_a.shape[0]

    def far_rows(i, carry):
        rows = pl.ds(pl.multiple_of(i * 16, 16), 16)
        x, y, z = points[0, rows], points[1, rows], points[2, rows]
        index = {}
        t = 0
        for a in range(DEGREE + 1):
            for b in range(DEGREE + 1 - a):
                for c in range(DEGREE + 1 - a - b):
                    index[a, b, c] = t
                    t += 1
        for d in range(3):
            in_x = None
            for a in range(DEGREE, -1, -1):
                in_y = None
                for b in range(DEGREE - a, -1, -1):
                    in_z = None
                    for c in range(DEGREE - a - b, -1, -1):
                        value = local[d, index[a, b, c]]
                        in_z = value if in_z is None else in_z * z + value
                    in_y = in_z if in_y is None else in_y * y + in_z
                in_x = in_y if in_x is None else in_x * x + in_y
            out[d, rows, :] = in_x[:, 0:count]
        return carry

    lax.fori_loop(0, cells // 16, far_rows, 0)

    row8 = lax.broadcasted_iota(jnp.int32, (8, 128), 0)
    lane8 = lax.broadcasted_iota(jnp.int32, (8, 128), 1)

    def take(n, data):
        last = jnp.zeros((8, 128), f32)
        for k in range(2):
            first, second = data[3 + 4 * k : 4 + 4 * k, 0:128], data[3 + 4 * k : 4 + 4 * k, 128:256]
            last = jnp.where(row8 == 4 * k, first, last)
            last = jnp.where(row8 == 4 * k + 1, pltpu.roll(first, 64, 1), last)
            last = jnp.where(row8 == 4 * k + 2, second, last)
        for d in range(3):
            at_centre = (row8 == d) & (lane8 == count - 256)
            last = jnp.where(at_centre, data[3:4, 192 + d : 193 + d], last)
        packed[n, :, 0:256] = data
        packed[n, :, 256:384] = last

    def list_slot(s, n):
        q, k = s // 2, lax.rem(s, 2)
        flag = live[0, k, q]

        @pl.when(flag > 0)
        def _():
            cell_list[n] = owner[0, k, q]
            take(n, got_b[q, k])

        n = n + jnp.where(flag > 0, 1, 0)
        flag_in = meta[0, 4 * q + 2 + k]

        @pl.when(flag_in > 0)
        def _():
            cell_list[n] = meta[0, 4 * q + k]
            take(n, got_a[q, k])

        return n + jnp.where(flag_in > 0, 1, 0)

    units = lax.fori_loop(0, 2 * n_cell, list_slot, jnp.int32(0))
    load.wait()

    up_high[...] = jnp.zeros_like(up_high)
    up_low[...] = jnp.zeros_like(up_low)
    whole = upsample[...]
    high = whole.astype(bf16)
    up_high[:, 0:up_count] = high
    up_low[:, 0:up_count] = (whole - high.astype(f32)).astype(bf16)

    def spread_units(i, carry):
        rows = pl.ds(i * 16, 16)
        data = packed[rows].reshape(128, LANES)[:, 0:count]
        first = data.astype(bf16)
        second = (data - first.astype(f32)).astype(bf16)
        result = (
            jnp.dot(first, up_high[...], preferred_element_type=f32)
            + jnp.dot(second, up_high[...], preferred_element_type=f32)
            + jnp.dot(first, up_low[...], preferred_element_type=f32)
        )
        spread[rows] = result.reshape(16, 8, UP_LANES)
        return carry

    lax.fori_loop(0, (units + 15) // 16, spread_units, 0)

    def build(u, carry):
        cell = cell_list[u]
        target = block[cell]
        row = lax.broadcasted_iota(jnp.int32, (8, UP_LANES), 0)
        between = packed[u][:, count : count + 1] - target[:, count : count + 1]
        z = jnp.where(row < 3, STRETCH * (spread[u] + between), spread[u])
        table[u] = z
        square = jnp.sum(jnp.where(row < 3, z * z, 0.0), axis=0, keepdims=True) + 1.0
        aligned = jnp.concatenate([z[4:8], z[0:4]], axis=0)
        product = jnp.sum(jnp.where(row < 3, z * aligned, 0.0), axis=0, keepdims=True)
        feature = jnp.where(row < 3, -2.0 * z, jnp.where(row == 3, square, jnp.where(row == 7, -product, z)))
        f1, f2, f3 = split3(feature)
        constant = jnp.where(row < 3, 1.0, 0.0)
        for k, pair in enumerate(((f1, f2), (f1, f3), (f2, f1), (constant, jnp.zeros_like(constant)))):
            right[u, 16 * k : 16 * k + 16] = jnp.concatenate(pair, axis=0).astype(bf16)

        small = lax.broadcasted_iota(jnp.int32, (8, LANES), 0)
        y = jnp.where(small < 3, STRETCH * target, 0.0)
        yy = jnp.sum(y * y, axis=0, keepdims=True)
        y1, y2, y3 = split3(y)
        s1, s2, s3 = split3(yy)
        one = jnp.where(small == 3, 1.0, y1)
        squares = jnp.where(small == 0, s1, jnp.where(small == 1, s2, jnp.where(small == 2, s3, 0.0)))
        zero = jnp.zeros_like(y)
        order = [one, one, y2, one, y2, y3]
        lower = [jnp.concatenate([v[4:8], v[0:4]], axis=0) for v in order]
        for k, rows in enumerate((order + [squares, zero], lower + [zero, zero])):
            turned = jnp.transpose(jnp.concatenate(rows, axis=0))
            left[u, k] = turned[0:count].astype(bf16)
        return carry

    lax.fori_loop(0, units, build, 0)

    columns[...] = jnp.zeros_like(columns)
    step = 40

    def one_unit(u, carry):
        cell = cell_list[u]
        for begin in range(0, count, step):
            size = min(step, count - begin)
            near = [jnp.zeros((size, 128), f32) for _ in range(4)]
            left_s = left[u, 0, begin : begin + size]
            left_p = left[u, 1, begin : begin + size]
            for c in range(UP_LANES // 128):
                lanes = slice(c * 128, c * 128 + 128)
                feature = right[u, :, lanes]
                inverse = lax.rsqrt(jnp.dot(left_s, feature, preferred_element_type=f32))
                projected = jnp.dot(left_p, feature, preferred_element_type=f32)
                cube = inverse * inverse * inverse
                along = inverse + cube
                across = cube * projected
                for d in range(3):
                    near[d] = near[d] + (
                        along * table[u, 4 + d : 5 + d, lanes] - across * table[u, d : d + 1, lanes]
                    )
                near[3] = near[3] + across
            for d in range(4):
                columns[begin : begin + size, d : d + 1] = jnp.sum(near[d], axis=1, keepdims=True)
        sums = jnp.transpose(columns[...])[0:8]
        small = lax.broadcasted_iota(jnp.int32, (8, LANES), 0)
        y = jnp.where(small < 3, STRETCH * block[cell], 0.0)
        velocity = (sums + y * sums[3:4]) * (STRETCH / up_count)
        for d in range(3):
            out[d, pl.ds(cell, 1), :] += velocity[d : d + 1, 0:count]
        return carry

    lax.fori_loop(0, units, one_unit, 0)


def on_device(centers, offsets, forces, upsample, translate, owner_cell, peer_cell, live):
    cells, count = offsets.shape[1], offsets.shape[2]
    n_cell = owner_cell.shape[1]
    vmem = pl.BlockSpec(memory_space=pltpu.VMEM)
    smem = pl.BlockSpec(memory_space=pltpu.SMEM)
    hbm = pl.BlockSpec(memory_space=pltpu.HBM)
    got = (n_cell, 2, 8, 256)
    owner, peer, live = (jnp.transpose(v, (0, 2, 1)) for v in (owner_cell, peer_cell, live))
    got_a, got_b, meta, block, points, local = pl.pallas_call(
        exchange_kernel,
        out_shape=(
            jax.ShapeDtypeStruct(got, f32),
            jax.ShapeDtypeStruct(got, f32),
            jax.ShapeDtypeStruct((1, 128), jnp.int32),
            jax.ShapeDtypeStruct((cells, 8, LANES), f32),
            jax.ShapeDtypeStruct((3, cells, LANES), f32),
            jax.ShapeDtypeStruct((3, NT), f32),
        ),
        in_specs=[smem] * 3 + [hbm] * 4,
        out_specs=(vmem,) * 6,
        scratch_shapes=[
            pltpu.VMEM(centers.shape, f32),
            pltpu.VMEM(offsets.shape, f32),
            pltpu.VMEM(forces.shape, f32),
            pltpu.VMEM(translate.shape, f32),
            pltpu.VMEM((cells, 8, 256), f32),
            pltpu.VMEM(got, f32),
            pltpu.VMEM(got, f32),
            pltpu.VMEM((n_cell, 8, 128), jnp.int32),
            pltpu.VMEM((n_cell, 8, 128), jnp.int32),
            pltpu.VMEM((1, 128), jnp.int32),
            pltpu.SMEM((1, 128), jnp.int32),
            pltpu.VMEM((8, 256), f32),
            pltpu.VMEM((n_cell, 8, 256), f32),
            pltpu.VMEM((8, 256), f32),
            pltpu.VMEM((2, 8, 256), f32),
            pltpu.VMEM((6, cells, LANES), f32),
            pltpu.VMEM((3, 168, 8, 128), f32),
            pltpu.SemaphoreType.DMA((4,)),
            pltpu.SemaphoreType.DMA((4,)),
            pltpu.SemaphoreType.DMA((2,)),
            pltpu.SemaphoreType.DMA((2,)),
            pltpu.SemaphoreType.DMA((4,)),
        ],
        compiler_params=pltpu.CompilerParams(
            collective_id=0, has_side_effects=True, vmem_limit_bytes=60 * 1024 * 1024
        ),
        name="exchange",
    )(owner, peer, live, centers, offsets, forces, translate)
    return pl.pallas_call(
        field_kernel,
        out_shape=jax.ShapeDtypeStruct((3, cells, count), f32),
        in_specs=[smem] * 4 + [vmem] * 4 + [hbm],
        out_specs=vmem,
        scratch_shapes=[
            pltpu.SMEM((cells,), jnp.int32),
            pltpu.VMEM(upsample.shape, f32),
            pltpu.VMEM((cells, 8, LANES), f32),
            pltpu.VMEM((cells, 8, UP_LANES), f32),
            pltpu.VMEM((count, UP_LANES), bf16),
            pltpu.VMEM((count, UP_LANES), bf16),
            pltpu.VMEM((cells, 2, count, 64), bf16),
            pltpu.VMEM((cells, 64, UP_LANES), bf16),
            pltpu.VMEM((cells, 8, UP_LANES), f32),
            pltpu.VMEM((LANES, 128), f32),
            pltpu.SemaphoreType.DMA,
        ],
        compiler_params=pltpu.CompilerParams(vmem_limit_bytes=61 * 1024 * 1024),
        name="field",
    )(meta, owner, live, local, block, got_a, got_b, points, upsample)


def solution(mesh):
    return jax.shard_map(
        on_device,
        mesh=mesh,
        in_specs=(
            P(None, ("slab", "cell")),
            P(None, ("slab", "cell"), None),
            P(None, ("slab", "cell"), None),
            P(),
            P(),
            P(("slab", "cell"), None, None),
            P(("slab", "cell"), None, None),
            P(("slab", "cell"), None, None),
        ),
        out_specs=P(None, ("slab", "cell"), None),
        check_vma=False,
    )
```

```python
import functools
import math

import jax
import jax.numpy as jnp
from jax import lax
from jax.experimental import pallas as pl
from jax.experimental.pallas import tpu as pltpu
from jax.sharding import PartitionSpec as P

DEGREE = 8
NT = 165
SOFTEN = 0.0025
STRETCH = 20.0
LANES = 384
UP_LANES = 1280
f32 = jnp.float32
bf16 = jnp.bfloat16
MESH = pl.DeviceIdType.MESH
highest = lax.Precision.HIGHEST
NT_DIMS = (((1,), (1,)), ((), ()))


def split3(x):
    first = x.astype(bf16).astype(f32)
    rest = x - first
    second = rest.astype(bf16).astype(f32)
    third = (rest - second).astype(bf16).astype(f32)
    return first, second, third


def exchange_kernel(
    owner, peer, live, centers_hbm, offsets_hbm, forces_hbm, translate_hbm,
    got_a, got_b, meta, block, points, local,
    centers, offsets, forces, translate, sent, send_a, send_b, send_meta, got_meta, merged, meta_here,
    mom_out, mom_in, total, beside, padded, acc,
    send_sems, recv_sems, side_send, side_recv, here_sems,
):
    n_cell = lax.axis_size("cell")
    n_slab = lax.axis_size("slab")
    me = lax.axis_index("cell")
    slab = lax.axis_index("slab")
    above = lax.rem(slab + 1, n_slab)
    below = lax.rem(slab + n_slab - 1, n_slab)
    cells, count = offsets.shape[1], offsets.shape[2]

    barrier = pltpu.get_barrier_semaphore()
    pairs = ((centers_hbm, centers), (offsets_hbm, offsets), (forces_hbm, forces), (translate_hbm, translate))
    loads = [pltpu.make_async_copy(source, target, here_sems.at[k]) for k, (source, target) in enumerate(pairs)]
    for load in loads:
        load.start()

    def greet(j, carry):
        to = lax.rem(me + j, n_cell)
        pl.semaphore_signal(barrier, inc=1, device_id={"cell": to}, device_id_type=MESH)
        return carry

    lax.fori_loop(1, n_cell, greet, 0)
    for side in (above, below):
        pl.semaphore_signal(barrier, inc=1, device_id={"slab": side}, device_id_type=MESH)

    small = lax.broadcasted_iota(jnp.int32, (8, 128), 1) - 4 * me
    for q in range(n_cell):
        row = jnp.zeros((8, 128), jnp.int32)
        for k in range(2):
            row = jnp.where(small == k, peer[0, k, q], row)
            row = jnp.where(small == 2 + k, live[0, k, q], row)
        send_meta[q] = row

    for load in loads[:3]:
        load.wait()

    lane = lax.broadcasted_iota(jnp.int32, (cells, LANES), 1)
    tail_lane = lax.broadcasted_iota(jnp.int32, (cells, 128), 1)
    diag = lax.broadcasted_iota(jnp.int32, (cells, cells), 0) == lax.broadcasted_iota(jnp.int32, (cells, cells), 1)
    block[...] = jnp.zeros_like(block)
    tails = []
    middle = jnp.zeros((cells, 128), f32)
    for d in range(3):
        column = jnp.sum(jnp.where(diag, centers[d : d + 1, :], 0.0), axis=1, keepdims=True)
        padded[d, :, 0:count] = offsets[d]
        padded[3 + d, :, 0:count] = forces[d]
        offset = jnp.where(lane < count, padded[d], 0.0)
        force = jnp.where(lane < count, padded[3 + d], 0.0)
        block[:, d, :] = jnp.where(lane == count, column, offset)
        block[:, 4 + d, :] = force
        sent[:, d, :] = offset[:, 0:256]
        sent[:, 4 + d, :] = force[:, 0:256]
        padded[3 + d] = force
        points[d] = jnp.where(lane < count, offset + column, 0.0)
        tails.append((offset[:, 256:384], force[:, 256:384]))
        middle = jnp.where(tail_lane == 64 + d, column, middle)
    for k in range(2):
        sent[:, 3 + 4 * k, 0:128] = tails[0][k] + pltpu.roll(tails[1][k], 64, 1)
        sent[:, 3 + 4 * k, 128:256] = tails[2][k] + middle

    for q in range(n_cell):
        for k in range(2):
            send_a[q, k] = sent[owner[0, k, q]]

    pl.semaphore_wait(barrier, n_cell + 1)

    def send(kind, source, target):
        def step(j, carry):
            to = lax.rem(me + j, n_cell)
            pltpu.make_async_remote_copy(
                src_ref=source if kind == 3 else source.at[to],
                dst_ref=target.at[me],
                send_sem=send_sems.at[kind],
                recv_sem=recv_sems.at[kind],
                device_id={"cell": to},
                device_id_type=MESH,
            ).start()
            return carry

        lax.fori_loop(1, n_cell, step, 0)

    def every(kind, target):
        part = target.at[pl.ds(0, n_cell - 1)]
        return pltpu.make_async_remote_copy(
            src_ref=part,
            dst_ref=part,
            send_sem=send_sems.at[kind],
            recv_sem=recv_sems.at[kind],
            device_id={"cell": lax.rem(me + 1, n_cell)},
            device_id_type=MESH,
        )

    send(0, send_meta, got_meta)
    send(1, send_a, got_a)
    got_meta[me] = send_meta[me]
    got_a[me] = send_a[me]
    acc[...] = jnp.zeros_like(acc)

    def moment_rows(i, carry):
        rows = pl.ds(pl.multiple_of(i * 8, 8), 8)
        x, y, z = points[0, rows], points[1, rows], points[2, rows]
        force = [padded[3 + d, rows] for d in range(3)]
        t = 0
        power_x = jnp.ones_like(x)
        for a in range(DEGREE + 1):
            power_y = power_x
            for b in range(DEGREE + 1 - a):
                term = power_y
                for c in range(DEGREE + 1 - a - b):
                    for d in range(3):
                        v = term * force[d]
                        acc[d, t] += v[:, 0:128] + v[:, 128:256] + v[:, 256:384]
                    t += 1
                    if c < DEGREE - a - b:
                        term = term * z
                if b < DEGREE - a:
                    power_y = power_y * y
            if a < DEGREE:
                power_x = power_x * x
        return carry

    lax.fori_loop(0, cells // 8, moment_rows, 0)
    scale = 1.0 / math.sqrt(cells * n_cell * count)
    terms = acc.shape[1]
    sub = lax.broadcasted_iota(jnp.int32, (8, terms), 0)
    moments = jnp.zeros((8, terms), f32)
    for d in range(3):
        part = jnp.sum(acc[d], axis=1)
        row = lax.dot_general(jnp.ones((8, 128), f32), part, NT_DIMS, precision=highest, preferred_element_type=f32)
        moments = jnp.where(sub == d, row * scale, moments)
    mom_out[...] = jnp.zeros_like(mom_out)
    mom_out[:, 0:terms] = moments
    send(3, mom_out, mom_in)

    every(0, got_meta).wait_recv()
    whole = got_meta[0]
    for q in range(1, n_cell):
        whole = whole + got_meta[q]
    merged[...] = whole[0:1]
    meta[...] = whole[0:1]
    fetch = pltpu.make_async_copy(merged, meta_here, here_sems.at[0])
    fetch.start()
    fetch.wait()
    for q in range(n_cell):
        for k in range(2):
            send_b[q, k] = sent[meta_here[0, 4 * q + k]]
    send(2, send_b, got_b)
    got_b[me] = send_b[me]

    mom_in[me] = mom_out[...]
    every(3, mom_in).wait_recv()
    gathered = mom_in[0]
    for q in range(1, n_cell):
        gathered = gathered + mom_in[q]
    total[...] = gathered

    def side_copy(which, to):
        return pltpu.make_async_remote_copy(
            src_ref=total,
            dst_ref=beside.at[which],
            send_sem=side_send.at[which],
            recv_sem=side_recv.at[which],
            device_id={"slab": to},
            device_id_type=MESH,
        )

    up_copy, down_copy = side_copy(0, above), side_copy(1, below)
    up_copy.start()
    down_copy.start()
    up_copy.wait()
    down_copy.wait()
    lower = jnp.where(slab == 0, 0.0, beside[0])
    upper = jnp.where(slab == n_slab - 1, 0.0, beside[1])
    coef = jnp.zeros((8, NT), f32)
    loads[3].wait()
    for k, source in enumerate((total[...], lower, upper)):
        coef = coef + lax.dot_general(
            source[:, 0:NT], translate[k], NT_DIMS, precision=highest, preferred_element_type=f32
        )
    local[...] = coef[0:3]

    every(1, got_a).wait_recv()
    every(2, got_b).wait_recv()
    every(0, got_meta).wait_send()
    every(1, got_a).wait_send()
    every(2, got_b).wait_send()
    every(3, mom_in).wait_send()


def field_kernel(
    meta, owner, live, local, block, got_a, got_b, points, upsample_hbm,
    out,
    cell_list, upsample, packed, spread, up_high, up_low, left, right, table, columns, load_sem,
):
    load = pltpu.make_async_copy(upsample_hbm, upsample, load_sem)
    load.start()
    cells, count, up_count = out.shape[1], out.shape[2], upsample.shape[1]
    n_cell = got_a.shape[0]

    def far_rows(i, carry):
        rows = pl.ds(pl.multiple_of(i * 16, 16), 16)
        x, y, z = points[0, rows], points[1, rows], points[2, rows]
        index = {}
        t = 0
        for a in range(DEGREE + 1):
            for b in range(DEGREE + 1 - a):
                for c in range(DEGREE + 1 - a - b):
                    index[a, b, c] = t
                    t += 1
        for d in range(3):
            in_x = None
            for a in range(DEGREE, -1, -1):
                in_y = None
                for b in range(DEGREE - a, -1, -1):
                    in_z = None
                    for c in range(DEGREE - a - b, -1, -1):
                        value = local[d, index[a, b, c]]
                        in_z = value if in_z is None else in_z * z + value
                    in_y = in_z if in_y is None else in_y * y + in_z
                in_x = in_y if in_x is None else in_x * x + in_y
            out[d, rows, :] = in_x[:, 0:count]
        return carry

    lax.fori_loop(0, cells // 16, far_rows, 0)

    row8 = lax.broadcasted_iota(jnp.int32, (8, 128), 0)
    lane8 = lax.broadcasted_iota(jnp.int32, (8, 128), 1)

    def take(n, data):
        last = jnp.zeros((8, 128), f32)
        for k in range(2):
            first, second = data[3 + 4 * k : 4 + 4 * k, 0:128], data[3 + 4 * k : 4 + 4 * k, 128:256]
            last = jnp.where(row8 == 4 * k, first, last)
            last = jnp.where(row8 == 4 * k + 1, pltpu.roll(first, 64, 1), last)
            last = jnp.where(row8 == 4 * k + 2, second, last)
        for d in range(3):
            at_centre = (row8 == d) & (lane8 == count - 256)
            last = jnp.where(at_centre, data[3:4, 192 + d : 193 + d], last)
        packed[n, :, 0:256] = data
        packed[n, :, 256:384] = last

    def list_slot(s, n):
        q, k = s // 2, lax.rem(s, 2)
        flag = live[0, k, q]

        @pl.when(flag > 0)
        def _():
            cell_list[n] = owner[0, k, q]
            take(n, got_b[q, k])

        n = n + jnp.where(flag > 0, 1, 0)
        flag_in = meta[0, 4 * q + 2 + k]

        @pl.when(flag_in > 0)
        def _():
            cell_list[n] = meta[0, 4 * q + k]
            take(n, got_a[q, k])

        return n + jnp.where(flag_in > 0, 1, 0)

    units = lax.fori_loop(0, 2 * n_cell, list_slot, jnp.int32(0))
    load.wait()

    up_high[...] = jnp.zeros_like(up_high)
    up_low[...] = jnp.zeros_like(up_low)
    whole = upsample[...]
    high = whole.astype(bf16)
    up_high[:, 0:up_count] = high
    up_low[:, 0:up_count] = (whole - high.astype(f32)).astype(bf16)

    def spread_units(i, carry):
        rows = pl.ds(i * 16, 16)
        data = packed[rows].reshape(128, LANES)[:, 0:count]
        first = data.astype(bf16)
        second = (data - first.astype(f32)).astype(bf16)
        result = (
            jnp.dot(first, up_high[...], preferred_element_type=f32)
            + jnp.dot(second, up_high[...], preferred_element_type=f32)
            + jnp.dot(first, up_low[...], preferred_element_type=f32)
        )
        spread[rows] = result.reshape(16, 8, UP_LANES)
        return carry

    lax.fori_loop(0, (units + 15) // 16, spread_units, 0)

    def build(u, carry):
        cell = cell_list[u]
        target = block[cell]
        row = lax.broadcasted_iota(jnp.int32, (8, UP_LANES), 0)
        between = packed[u][:, count : count + 1] - target[:, count : count + 1]
        z = jnp.where(row < 3, STRETCH * (spread[u] + between), spread[u])
        table[u] = z
        square = jnp.sum(jnp.where(row < 3, z * z, 0.0), axis=0, keepdims=True) + 1.0
        aligned = jnp.concatenate([z[4:8], z[0:4]], axis=0)
        product = jnp.sum(jnp.where(row < 3, z * aligned, 0.0), axis=0, keepdims=True)
        feature = jnp.where(row < 3, -2.0 * z, jnp.where(row == 3, square, jnp.where(row == 7, -product, z)))
        f1, f2, f3 = split3(feature)
        constant = jnp.where(row < 3, 1.0, 0.0)
        for k, pair in enumerate(((f1, f2), (f1, f3), (f2, f1), (constant, jnp.zeros_like(constant)))):
            right[u, 16 * k : 16 * k + 16] = jnp.concatenate(pair, axis=0).astype(bf16)

        small = lax.broadcasted_iota(jnp.int32, (8, LANES), 0)
        y = jnp.where(small < 3, STRETCH * target, 0.0)
        yy = jnp.sum(y * y, axis=0, keepdims=True)
        y1, y2, y3 = split3(y)
        s1, s2, s3 = split3(yy)
        one = jnp.where(small == 3, 1.0, y1)
        squares = jnp.where(small == 0, s1, jnp.where(small == 1, s2, jnp.where(small == 2, s3, 0.0)))
        zero = jnp.zeros_like(y)
        order = [one, one, y2, one, y2, y3]
        lower = [jnp.concatenate([v[4:8], v[0:4]], axis=0) for v in order]
        for k, rows in enumerate((order + [squares, zero], lower + [zero, zero])):
            turned = jnp.transpose(jnp.concatenate(rows, axis=0))
            left[u, k] = turned[0:count].astype(bf16)
        return carry

    lax.fori_loop(0, units, build, 0)

    columns[...] = jnp.zeros_like(columns)
    step = 40

    def one_unit(u, carry):
        cell = cell_list[u]
        for begin in range(0, count, step):
            size = min(step, count - begin)
            near = [jnp.zeros((size, 128), f32) for _ in range(4)]
            left_s = left[u, 0, begin : begin + size]
            left_p = left[u, 1, begin : begin + size]
            for c in range(UP_LANES // 128):
                lanes = slice(c * 128, c * 128 + 128)
                feature = right[u, :, lanes]
                inverse = lax.rsqrt(jnp.dot(left_s, feature, preferred_element_type=f32))
                projected = jnp.dot(left_p, feature, preferred_element_type=f32)
                cube = inverse * inverse * inverse
                along = inverse + cube
                across = cube * projected
                for d in range(3):
                    near[d] = near[d] + (
                        along * table[u, 4 + d : 5 + d, lanes] - across * table[u, d : d + 1, lanes]
                    )
                near[3] = near[3] + across
            for d in range(4):
                columns[begin : begin + size, d : d + 1] = jnp.sum(near[d], axis=1, keepdims=True)
        sums = jnp.transpose(columns[...])[0:8]
        small = lax.broadcasted_iota(jnp.int32, (8, LANES), 0)
        y = jnp.where(small < 3, STRETCH * block[cell], 0.0)
        velocity = (sums + y * sums[3:4]) * (STRETCH / up_count)
        for d in range(3):
            out[d, pl.ds(cell, 1), :] += velocity[d : d + 1, 0:count]
        return carry

    lax.fori_loop(0, units, one_unit, 0)


def on_device(centers, offsets, forces, upsample, translate, owner_cell, peer_cell, live):
    cells, count = offsets.shape[1], offsets.shape[2]
    n_cell = owner_cell.shape[1]
    vmem = pl.BlockSpec(memory_space=pltpu.VMEM)
    smem = pl.BlockSpec(memory_space=pltpu.SMEM)
    hbm = pl.BlockSpec(memory_space=pltpu.HBM)
    got = (n_cell, 2, 8, 256)
    owner, peer, live = (jnp.transpose(v, (0, 2, 1)) for v in (owner_cell, peer_cell, live))
    got_a, got_b, meta, block, points, local = pl.pallas_call(
        exchange_kernel,
        out_shape=(
            jax.ShapeDtypeStruct(got, f32),
            jax.ShapeDtypeStruct(got, f32),
            jax.ShapeDtypeStruct((1, 128), jnp.int32),
            jax.ShapeDtypeStruct((cells, 8, LANES), f32),
            jax.ShapeDtypeStruct((3, cells, LANES), f32),
            jax.ShapeDtypeStruct((3, NT), f32),
        ),
        in_specs=[smem] * 3 + [hbm] * 4,
        out_specs=(vmem,) * 6,
        scratch_shapes=[
            pltpu.VMEM(centers.shape, f32),
            pltpu.VMEM(offsets.shape, f32),
            pltpu.VMEM(forces.shape, f32),
            pltpu.VMEM(translate.shape, f32),
            pltpu.VMEM((cells, 8, 256), f32),
            pltpu.VMEM(got, f32),
            pltpu.VMEM(got, f32),
            pltpu.VMEM((n_cell, 8, 128), jnp.int32),
            pltpu.VMEM((n_cell, 8, 128), jnp.int32),
            pltpu.VMEM((1, 128), jnp.int32),
            pltpu.SMEM((1, 128), jnp.int32),
            pltpu.VMEM((8, 256), f32),
            pltpu.VMEM((n_cell, 8, 256), f32),
            pltpu.VMEM((8, 256), f32),
            pltpu.VMEM((2, 8, 256), f32),
            pltpu.VMEM((6, cells, LANES), f32),
            pltpu.VMEM((3, 168, 8, 128), f32),
            pltpu.SemaphoreType.DMA((4,)),
            pltpu.SemaphoreType.DMA((4,)),
            pltpu.SemaphoreType.DMA((2,)),
            pltpu.SemaphoreType.DMA((2,)),
            pltpu.SemaphoreType.DMA((4,)),
        ],
        compiler_params=pltpu.CompilerParams(
            collective_id=0, has_side_effects=True, vmem_limit_bytes=60 * 1024 * 1024
        ),
        name="exchange",
    )(owner, peer, live, centers, offsets, forces, translate)
    return pl.pallas_call(
        field_kernel,
        out_shape=jax.ShapeDtypeStruct((3, cells, count), f32),
        in_specs=[smem] * 4 + [vmem] * 4 + [hbm],
        out_specs=vmem,
        scratch_shapes=[
            pltpu.SMEM((cells,), jnp.int32),
            pltpu.VMEM(upsample.shape, f32),
            pltpu.VMEM((cells, 8, LANES), f32),
            pltpu.VMEM((cells, 8, UP_LANES), f32),
            pltpu.VMEM((count, UP_LANES), bf16),
            pltpu.VMEM((count, UP_LANES), bf16),
            pltpu.VMEM((cells, 2, count, 64), bf16),
            pltpu.VMEM((cells, 64, UP_LANES), bf16),
            pltpu.VMEM((cells, 8, UP_LANES), f32),
            pltpu.VMEM((LANES, 128), f32),
            pltpu.SemaphoreType.DMA,
        ],
        compiler_params=pltpu.CompilerParams(vmem_limit_bytes=61 * 1024 * 1024),
        name="field",
    )(meta, owner, live, local, block, got_a, got_b, points, upsample)


def solution(mesh):
    return jax.shard_map(
        on_device,
        mesh=mesh,
        in_specs=(
            P(None, ("slab", "cell")),
            P(None, ("slab", "cell"), None),
            P(None, ("slab", "cell"), None),
            P(),
            P(),
            P(("slab", "cell"), None, None),
            P(("slab", "cell"), None, None),
            P(("slab", "cell"), None, None),
        ),
        out_specs=P(None, ("slab", "cell"), None),
        check_vma=False,
    )
```

```python
import functools
import math

import jax
import jax.numpy as jnp
from jax import lax
from jax.experimental import pallas as pl
from jax.experimental.pallas import tpu as pltpu
from jax.sharding import PartitionSpec as P

DEGREE = 8
NT = 165
SOFTEN = 0.0025
STRETCH = 20.0
LANES = 384
UP_LANES = 1280
f32 = jnp.float32
bf16 = jnp.bfloat16
MESH = pl.DeviceIdType.MESH
highest = lax.Precision.HIGHEST
NT_DIMS = (((1,), (1,)), ((), ()))


def split3(x):
    first = x.astype(bf16).astype(f32)
    rest = x - first
    second = rest.astype(bf16).astype(f32)
    third = (rest - second).astype(bf16).astype(f32)
    return first, second, third


def exchange_kernel(
    owner, peer, live, centers_hbm, offsets_hbm, forces_hbm, translate_hbm,
    got, meta, block, points, local,
    centers, offsets, forces, translate, sent, send_a, send_b, send_meta, got_meta, merged, meta_here,
    mom_out, mom_in, total, beside, padded, acc,
    send_sems, recv_sems, side_send, side_recv, here_sems,
):
    n_cell = lax.axis_size("cell")
    n_slab = lax.axis_size("slab")
    me = lax.axis_index("cell")
    slab = lax.axis_index("slab")
    above = lax.rem(slab + 1, n_slab)
    below = lax.rem(slab + n_slab - 1, n_slab)
    cells, count = offsets.shape[1], offsets.shape[2]

    got_a, got_b = got.at[0], got.at[1]
    barrier = pltpu.get_barrier_semaphore()
    pairs = ((centers_hbm, centers), (offsets_hbm, offsets), (forces_hbm, forces), (translate_hbm, translate))
    loads = [pltpu.make_async_copy(source, target, here_sems.at[k]) for k, (source, target) in enumerate(pairs)]
    for load in loads:
        load.start()

    def greet(j, carry):
        to = lax.rem(me + j, n_cell)
        pl.semaphore_signal(barrier, inc=1, device_id={"cell": to}, device_id_type=MESH)
        return carry

    lax.fori_loop(1, n_cell, greet, 0)
    for side in (above, below):
        pl.semaphore_signal(barrier, inc=1, device_id={"slab": side}, device_id_type=MESH)

    small = lax.broadcasted_iota(jnp.int32, (8, 128), 1) - 4 * me
    for q in range(n_cell):
        row = jnp.zeros((8, 128), jnp.int32)
        for k in range(2):
            row = jnp.where(small == k, peer[0, k, q], row)
            row = jnp.where(small == 2 + k, live[0, k, q], row)
        send_meta[q] = row

    for load in loads[:3]:
        load.wait()

    lane = lax.broadcasted_iota(jnp.int32, (cells, LANES), 1)
    tail_lane = lax.broadcasted_iota(jnp.int32, (cells, 128), 1)
    diag = lax.broadcasted_iota(jnp.int32, (cells, cells), 0) == lax.broadcasted_iota(jnp.int32, (cells, cells), 1)
    block[...] = jnp.zeros_like(block)
    tails = []
    middle = jnp.zeros((cells, 128), f32)
    for d in range(3):
        column = jnp.sum(jnp.where(diag, centers[d : d + 1, :], 0.0), axis=1, keepdims=True)
        padded[d, :, 0:count] = offsets[d]
        padded[3 + d, :, 0:count] = forces[d]
        offset = jnp.where(lane < count, padded[d], 0.0)
        force = jnp.where(lane < count, padded[3 + d], 0.0)
        block[:, d, :] = jnp.where(lane == count, column, offset)
        block[:, 4 + d, :] = force
        sent[:, d, :] = offset[:, 0:256]
        sent[:, 4 + d, :] = force[:, 0:256]
        padded[3 + d] = force
        points[d] = jnp.where(lane < count, offset + column, 0.0)
        tails.append((offset[:, 256:384], force[:, 256:384]))
        middle = jnp.where(tail_lane == 64 + d, column, middle)
    for k in range(2):
        sent[:, 3 + 4 * k, 0:128] = tails[0][k] + pltpu.roll(tails[1][k], 64, 1)
        sent[:, 3 + 4 * k, 128:256] = tails[2][k] + middle

    for q in range(n_cell):
        for k in range(2):
            send_a[q, k] = sent[owner[0, k, q]]

    pl.semaphore_wait(barrier, n_cell + 1)

    def send(kind, source, target):
        def step(j, carry):
            to = lax.rem(me + j, n_cell)
            pltpu.make_async_remote_copy(
                src_ref=source if kind == 3 else source.at[to],
                dst_ref=target.at[me],
                send_sem=send_sems.at[kind],
                recv_sem=recv_sems.at[kind],
                device_id={"cell": to},
                device_id_type=MESH,
            ).start()
            return carry

        lax.fori_loop(1, n_cell, step, 0)

    def every(kind, target):
        part = target.at[pl.ds(0, n_cell - 1)]
        return pltpu.make_async_remote_copy(
            src_ref=part,
            dst_ref=part,
            send_sem=send_sems.at[kind],
            recv_sem=recv_sems.at[kind],
            device_id={"cell": lax.rem(me + 1, n_cell)},
            device_id_type=MESH,
        )

    send(0, send_meta, got_meta)
    send(1, send_a, got_a)
    got_meta[me] = send_meta[me]
    got_a[me] = send_a[me]
    acc[...] = jnp.zeros_like(acc)

    def moment_rows(i, carry):
        rows = pl.ds(pl.multiple_of(i * 8, 8), 8)
        x, y, z = points[0, rows], points[1, rows], points[2, rows]
        force = [padded[3 + d, rows] for d in range(3)]
        t = 0
        power_x = jnp.ones_like(x)
        for a in range(DEGREE + 1):
            power_y = power_x
            for b in range(DEGREE + 1 - a):
                term = power_y
                for c in range(DEGREE + 1 - a - b):
                    for d in range(3):
                        v = term * force[d]
                        acc[d, t] += v[:, 0:128] + v[:, 128:256] + v[:, 256:384]
                    t += 1
                    if c < DEGREE - a - b:
                        term = term * z
                if b < DEGREE - a:
                    power_y = power_y * y
            if a < DEGREE:
                power_x = power_x * x
        return carry

    lax.fori_loop(0, cells // 8, moment_rows, 0)
    scale = 1.0 / math.sqrt(cells * n_cell * count)
    terms = acc.shape[1]
    sub = lax.broadcasted_iota(jnp.int32, (8, terms), 0)
    moments = jnp.zeros((8, terms), f32)
    for d in range(3):
        part = jnp.sum(acc[d], axis=1)
        row = lax.dot_general(jnp.ones((8, 128), f32), part, NT_DIMS, precision=highest, preferred_element_type=f32)
        moments = jnp.where(sub == d, row * scale, moments)
    mom_out[...] = jnp.zeros_like(mom_out)
    mom_out[:, 0:terms] = moments
    send(3, mom_out, mom_in)

    every(0, got_meta).wait_recv()
    whole = got_meta[0]
    for q in range(1, n_cell):
        whole = whole + got_meta[q]
    merged[...] = whole[0:1]
    meta[...] = whole[0:1]
    fetch = pltpu.make_async_copy(merged, meta_here, here_sems.at[0])
    fetch.start()
    fetch.wait()
    for q in range(n_cell):
        for k in range(2):
            send_b[q, k] = sent[meta_here[0, 4 * q + k]]
    send(2, send_b, got_b)
    got_b[me] = send_b[me]

    mom_in[me] = mom_out[...]
    every(3, mom_in).wait_recv()
    gathered = mom_in[0]
    for q in range(1, n_cell):
        gathered = gathered + mom_in[q]
    total[...] = gathered

    def side_copy(which, to):
        return pltpu.make_async_remote_copy(
            src_ref=total,
            dst_ref=beside.at[which],
            send_sem=side_send.at[which],
            recv_sem=side_recv.at[which],
            device_id={"slab": to},
            device_id_type=MESH,
        )

    up_copy, down_copy = side_copy(0, above), side_copy(1, below)
    up_copy.start()
    down_copy.start()
    up_copy.wait()
    down_copy.wait()
    lower = jnp.where(slab == 0, 0.0, beside[0])
    upper = jnp.where(slab == n_slab - 1, 0.0, beside[1])
    coef = jnp.zeros((8, NT), f32)
    loads[3].wait()
    for k, source in enumerate((total[...], lower, upper)):
        coef = coef + lax.dot_general(
            source[:, 0:NT], translate[k], NT_DIMS, precision=highest, preferred_element_type=f32
        )
    local[...] = coef[0:3]

    every(1, got_a).wait_recv()
    every(2, got_b).wait_recv()
    every(0, got_meta).wait_send()
    every(1, got_a).wait_send()
    every(2, got_b).wait_send()
    every(3, mom_in).wait_send()


def field_kernel(
    meta, owner, live, local, block, got, points, upsample_hbm,
    out,
    cell_list, source_list, upsample, packed, spread, up_high, up_low, left, right, table, columns, load_sem,
):
    load = pltpu.make_async_copy(upsample_hbm, upsample, load_sem)
    load.start()
    cells, count, up_count = out.shape[1], out.shape[2], upsample.shape[1]
    n_cell = owner.shape[2]

    def far_rows(i, carry):
        rows = pl.ds(pl.multiple_of(i * 16, 16), 16)
        x, y, z = points[0, rows], points[1, rows], points[2, rows]
        index = {}
        t = 0
        for a in range(DEGREE + 1):
            for b in range(DEGREE + 1 - a):
                for c in range(DEGREE + 1 - a - b):
                    index[a, b, c] = t
                    t += 1
        for d in range(3):
            in_x = None
            for a in range(DEGREE, -1, -1):
                in_y = None
                for b in range(DEGREE - a, -1, -1):
                    in_z = None
                    for c in range(DEGREE - a - b, -1, -1):
                        value = local[d, index[a, b, c]]
                        in_z = value if in_z is None else in_z * z + value
                    in_y = in_z if in_y is None else in_y * y + in_z
                in_x = in_y if in_x is None else in_x * x + in_y
            out[d, rows, :] = in_x[:, 0:count]
        return carry

    lax.fori_loop(0, cells // 16, far_rows, 0)

    row8 = lax.broadcasted_iota(jnp.int32, (8, 128), 0)
    lane8 = lax.broadcasted_iota(jnp.int32, (8, 128), 1)

    def take(n, data):
        last = jnp.zeros((8, 128), f32)
        for k in range(2):
            first, second = data[3 + 4 * k : 4 + 4 * k, 0:128], data[3 + 4 * k : 4 + 4 * k, 128:256]
            last = jnp.where(row8 == 4 * k, first, last)
            last = jnp.where(row8 == 4 * k + 1, pltpu.roll(first, 64, 1), last)
            last = jnp.where(row8 == 4 * k + 2, second, last)
        for d in range(3):
            at_centre = (row8 == d) & (lane8 == count - 256)
            last = jnp.where(at_centre, data[3:4, 192 + d : 193 + d], last)
        packed[n, :, 0:256] = data
        packed[n, :, 256:384] = last

    def clear(n, carry):
        cell_list[n] = 0
        source_list[n] = 0
        return carry

    lax.fori_loop(0, cells, clear, 0)

    def list_slot(q, n):
        for k in range(2):
            cell_list[n] = owner[0, k, q]
            source_list[n] = 2 * n_cell + 2 * q + k
            n = n + live[0, k, q]
            cell_list[n] = meta[0, 4 * q + k]
            source_list[n] = 2 * q + k
            n = n + meta[0, 4 * q + 2 + k]
        return n

    units = lax.fori_loop(0, n_cell, list_slot, jnp.int32(0))
    load.wait()

    up_high[...] = jnp.zeros_like(up_high)
    up_low[...] = jnp.zeros_like(up_low)
    whole = upsample[...]
    high = whole.astype(bf16)
    up_high[:, 0:up_count] = high
    up_low[:, 0:up_count] = (whole - high.astype(f32)).astype(bf16)

    def spread_units(i, carry):
        rows = pl.ds(i * 16, 16)
        for k in range(16):
            take(i * 16 + k, got[source_list[i * 16 + k]])
        data = packed[rows].reshape(128, LANES)[:, 0:count]
        first = data.astype(bf16)
        second = (data - first.astype(f32)).astype(bf16)
        result = (
            jnp.dot(first, up_high[...], preferred_element_type=f32)
            + jnp.dot(second, up_high[...], preferred_element_type=f32)
            + jnp.dot(first, up_low[...], preferred_element_type=f32)
        )
        spread[rows] = result.reshape(16, 8, UP_LANES)
        return carry

    lax.fori_loop(0, (units + 15) // 16, spread_units, 0)

    def build(u):
        cell = cell_list[u]
        target = block[cell]
        row = lax.broadcasted_iota(jnp.int32, (8, UP_LANES), 0)
        between = packed[u][:, count : count + 1] - target[:, count : count + 1]
        z = jnp.where(row < 3, STRETCH * (spread[u] + between), spread[u])
        table[u] = z
        square = jnp.sum(jnp.where(row < 3, z * z, 0.0), axis=0, keepdims=True) + 1.0
        aligned = jnp.concatenate([z[4:8], z[0:4]], axis=0)
        product = jnp.sum(jnp.where(row < 3, z * aligned, 0.0), axis=0, keepdims=True)
        feature = jnp.where(row < 3, -2.0 * z, jnp.where(row == 3, square, jnp.where(row == 7, -product, z)))
        f1, f2, f3 = split3(feature)
        constant = jnp.where(row < 3, 1.0, 0.0)
        for k, pair in enumerate(((f1, f2), (f1, f3), (f2, f1), (constant, jnp.zeros_like(constant)))):
            right[u, 16 * k : 16 * k + 16] = jnp.concatenate(pair, axis=0).astype(bf16)

        small = lax.broadcasted_iota(jnp.int32, (8, LANES), 0)
        y = jnp.where(small < 3, STRETCH * target, 0.0)
        yy = jnp.sum(y * y, axis=0, keepdims=True)
        y1, y2, y3 = split3(y)
        s1, s2, s3 = split3(yy)
        one = jnp.where(small == 3, 1.0, y1)
        squares = jnp.where(small == 0, s1, jnp.where(small == 1, s2, jnp.where(small == 2, s3, 0.0)))
        zero = jnp.zeros_like(y)
        order = [one, one, y2, one, y2, y3]
        lower = [jnp.concatenate([v[4:8], v[0:4]], axis=0) for v in order]
        for k, rows in enumerate((order + [squares, zero], lower + [zero, zero])):
            turned = jnp.transpose(jnp.concatenate(rows, axis=0))
            left[u, k] = turned[0:count].astype(bf16)

    def build_two(i, carry):
        build(2 * i)
        build(2 * i + 1)
        return carry

    lax.fori_loop(0, (units + 1) // 2, build_two, 0)

    columns[...] = jnp.zeros_like(columns)
    step = 40

    def one_unit(u, carry):
        cell = cell_list[u]
        for begin in range(0, count, step):
            size = min(step, count - begin)
            near = [jnp.zeros((size, 128), f32) for _ in range(4)]
            left_s = left[u, 0, begin : begin + size]
            left_p = left[u, 1, begin : begin + size]
            for c in range(UP_LANES // 128):
                lanes = slice(c * 128, c * 128 + 128)
                feature = right[u, :, lanes]
                inverse = lax.rsqrt(jnp.dot(left_s, feature, preferred_element_type=f32))
                projected = jnp.dot(left_p, feature, preferred_element_type=f32)
                cube = inverse * inverse * inverse
                along = inverse + cube
                across = cube * projected
                for d in range(3):
                    near[d] = near[d] + (
                        along * table[u, 4 + d : 5 + d, lanes] - across * table[u, d : d + 1, lanes]
                    )
                near[3] = near[3] + across
            for d in range(4):
                columns[begin : begin + size, d : d + 1] = jnp.sum(near[d], axis=1, keepdims=True)
        sums = jnp.transpose(columns[...])[0:8]
        small = lax.broadcasted_iota(jnp.int32, (8, LANES), 0)
        y = jnp.where(small < 3, STRETCH * block[cell], 0.0)
        velocity = (sums + y * sums[3:4]) * (STRETCH / up_count)
        for d in range(3):
            out[d, pl.ds(cell, 1), :] += velocity[d : d + 1, 0:count]
        return carry

    lax.fori_loop(0, units, one_unit, 0)


def on_device(centers, offsets, forces, upsample, translate, owner_cell, peer_cell, live):
    cells, count = offsets.shape[1], offsets.shape[2]
    n_cell = owner_cell.shape[1]
    vmem = pl.BlockSpec(memory_space=pltpu.VMEM)
    smem = pl.BlockSpec(memory_space=pltpu.SMEM)
    hbm = pl.BlockSpec(memory_space=pltpu.HBM)
    slots = (n_cell, 2, 8, 256)
    owner, peer, live = (jnp.transpose(v, (0, 2, 1)) for v in (owner_cell, peer_cell, live))
    got, meta, block, points, local = pl.pallas_call(
        exchange_kernel,
        out_shape=(
            jax.ShapeDtypeStruct((2,) + slots, f32),
            jax.ShapeDtypeStruct((1, 128), jnp.int32),
            jax.ShapeDtypeStruct((cells, 8, LANES), f32),
            jax.ShapeDtypeStruct((3, cells, LANES), f32),
            jax.ShapeDtypeStruct((3, NT), f32),
        ),
        in_specs=[smem] * 3 + [hbm] * 4,
        out_specs=(vmem,) * 5,
        scratch_shapes=[
            pltpu.VMEM(centers.shape, f32),
            pltpu.VMEM(offsets.shape, f32),
            pltpu.VMEM(forces.shape, f32),
            pltpu.VMEM(translate.shape, f32),
            pltpu.VMEM((cells, 8, 256), f32),
            pltpu.VMEM(slots, f32),
            pltpu.VMEM(slots, f32),
            pltpu.VMEM((n_cell, 8, 128), jnp.int32),
            pltpu.VMEM((n_cell, 8, 128), jnp.int32),
            pltpu.VMEM((1, 128), jnp.int32),
            pltpu.SMEM((1, 128), jnp.int32),
            pltpu.VMEM((8, 256), f32),
            pltpu.VMEM((n_cell, 8, 256), f32),
            pltpu.VMEM((8, 256), f32),
            pltpu.VMEM((2, 8, 256), f32),
            pltpu.VMEM((6, cells, LANES), f32),
            pltpu.VMEM((3, 168, 8, 128), f32),
            pltpu.SemaphoreType.DMA((4,)),
            pltpu.SemaphoreType.DMA((4,)),
            pltpu.SemaphoreType.DMA((2,)),
            pltpu.SemaphoreType.DMA((2,)),
            pltpu.SemaphoreType.DMA((4,)),
        ],
        compiler_params=pltpu.CompilerParams(
            collective_id=0, has_side_effects=True, vmem_limit_bytes=60 * 1024 * 1024
        ),
        name="exchange",
    )(owner, peer, live, centers, offsets, forces, translate)
    return pl.pallas_call(
        field_kernel,
        out_shape=jax.ShapeDtypeStruct((3, cells, count), f32),
        in_specs=[smem] * 4 + [vmem] * 3 + [hbm],
        out_specs=vmem,
        scratch_shapes=[
            pltpu.SMEM((cells + 1,), jnp.int32),
            pltpu.SMEM((cells + 1,), jnp.int32),
            pltpu.VMEM(upsample.shape, f32),
            pltpu.VMEM((cells, 8, LANES), f32),
            pltpu.VMEM((cells, 8, UP_LANES), f32),
            pltpu.VMEM((count, UP_LANES), bf16),
            pltpu.VMEM((count, UP_LANES), bf16),
            pltpu.VMEM((cells, 2, count, 64), bf16),
            pltpu.VMEM((cells, 64, UP_LANES), bf16),
            pltpu.VMEM((cells, 8, UP_LANES), f32),
            pltpu.VMEM((LANES, 128), f32),
            pltpu.SemaphoreType.DMA,
        ],
        compiler_params=pltpu.CompilerParams(vmem_limit_bytes=61 * 1024 * 1024),
        name="field",
    )(meta, owner, live, local, block, got.reshape(4 * n_cell, 8, 256), points, upsample)


def solution(mesh):
    return jax.shard_map(
        on_device,
        mesh=mesh,
        in_specs=(
            P(None, ("slab", "cell")),
            P(None, ("slab", "cell"), None),
            P(None, ("slab", "cell"), None),
            P(),
            P(),
            P(("slab", "cell"), None, None),
            P(("slab", "cell"), None, None),
            P(("slab", "cell"), None, None),
        ),
        out_specs=P(None, ("slab", "cell"), None),
        check_vma=False,
    )
```

```python
import functools
import math

import jax
import jax.numpy as jnp
from jax import lax
from jax.experimental import pallas as pl
from jax.experimental.pallas import tpu as pltpu
from jax.sharding import PartitionSpec as P

DEGREE = 8
NT = 165
SOFTEN = 0.0025
STRETCH = 20.0
LANES = 384
UP_LANES = 1280
f32 = jnp.float32
bf16 = jnp.bfloat16
MESH = pl.DeviceIdType.MESH
highest = lax.Precision.HIGHEST
NT_DIMS = (((1,), (1,)), ((), ()))


def split3(x):
    first = x.astype(bf16).astype(f32)
    rest = x - first
    second = rest.astype(bf16).astype(f32)
    third = (rest - second).astype(bf16).astype(f32)
    return first, second, third


def exchange_kernel(
    owner, peer, live, centers_hbm, offsets_hbm, forces_hbm, translate_hbm,
    got, meta, block, points, local,
    centers, offsets, forces, translate, sent, send_a, send_b, send_meta, got_meta, merged, meta_here,
    mom_out, mom_in, total, beside, padded, acc,
    send_sems, recv_sems, side_send, side_recv, here_sems,
):
    n_cell = lax.axis_size("cell")
    n_slab = lax.axis_size("slab")
    me = lax.axis_index("cell")
    slab = lax.axis_index("slab")
    above = lax.rem(slab + 1, n_slab)
    below = lax.rem(slab + n_slab - 1, n_slab)
    cells, count = offsets.shape[1], offsets.shape[2]

    got_a, got_b = got.at[0], got.at[1]
    barrier = pltpu.get_barrier_semaphore()
    pairs = ((centers_hbm, centers), (offsets_hbm, offsets), (forces_hbm, forces), (translate_hbm, translate))
    loads = [pltpu.make_async_copy(source, target, here_sems.at[k]) for k, (source, target) in enumerate(pairs)]
    for load in loads:
        load.start()

    def greet(j, carry):
        to = lax.rem(me + j, n_cell)
        pl.semaphore_signal(barrier, inc=1, device_id={"cell": to}, device_id_type=MESH)
        return carry

    lax.fori_loop(1, n_cell, greet, 0)
    for side in (above, below):
        pl.semaphore_signal(barrier, inc=1, device_id={"slab": side}, device_id_type=MESH)

    small = lax.broadcasted_iota(jnp.int32, (8, 128), 1) - 4 * me
    for q in range(n_cell):
        row = jnp.zeros((8, 128), jnp.int32)
        for k in range(2):
            row = jnp.where(small == k, peer[0, k, q], row)
            row = jnp.where(small == 2 + k, live[0, k, q], row)
        send_meta[q] = row

    for load in loads[:3]:
        load.wait()

    lane = lax.broadcasted_iota(jnp.int32, (cells, LANES), 1)
    tail_lane = lax.broadcasted_iota(jnp.int32, (cells, 128), 1)
    diag = lax.broadcasted_iota(jnp.int32, (cells, cells), 0) == lax.broadcasted_iota(jnp.int32, (cells, cells), 1)
    block[...] = jnp.zeros_like(block)
    tails = []
    middle = jnp.zeros((cells, 128), f32)
    for d in range(3):
        column = jnp.sum(jnp.where(diag, centers[d : d + 1, :], 0.0), axis=1, keepdims=True)
        padded[d, :, 0:count] = offsets[d]
        padded[3 + d, :, 0:count] = forces[d]
        offset = jnp.where(lane < count, padded[d], 0.0)
        force = jnp.where(lane < count, padded[3 + d], 0.0)
        block[:, d, :] = jnp.where(lane == count, column, offset)
        block[:, 4 + d, :] = force
        sent[:, d, :] = offset[:, 0:256]
        sent[:, 4 + d, :] = force[:, 0:256]
        padded[3 + d] = force
        points[d] = jnp.where(lane < count, offset + column, 0.0)
        tails.append((offset[:, 256:384], force[:, 256:384]))
        middle = jnp.where(tail_lane == 64 + d, column, middle)
    for k in range(2):
        sent[:, 3 + 4 * k, 0:128] = tails[0][k] + pltpu.roll(tails[1][k], 64, 1)
        sent[:, 3 + 4 * k, 128:256] = tails[2][k] + middle

    for q in range(n_cell):
        for k in range(2):
            send_a[q, k] = sent[owner[0, k, q]]

    pl.semaphore_wait(barrier, n_cell + 1)

    def send(kind, source, target):
        def step(j, carry):
            to = lax.rem(me + j, n_cell)
            pltpu.make_async_remote_copy(
                src_ref=source if kind == 3 else source.at[to],
                dst_ref=target.at[me],
                send_sem=send_sems.at[kind],
                recv_sem=recv_sems.at[kind],
                device_id={"cell": to},
                device_id_type=MESH,
            ).start()
            return carry

        lax.fori_loop(1, n_cell, step, 0)

    def every(kind, target):
        part = target.at[pl.ds(0, n_cell - 1)]
        return pltpu.make_async_remote_copy(
            src_ref=part,
            dst_ref=part,
            send_sem=send_sems.at[kind],
            recv_sem=recv_sems.at[kind],
            device_id={"cell": lax.rem(me + 1, n_cell)},
            device_id_type=MESH,
        )

    send(0, send_meta, got_meta)
    send(1, send_a, got_a)
    got_meta[me] = send_meta[me]
    got_a[me] = send_a[me]
    acc[...] = jnp.zeros_like(acc)

    def moment_rows(i, carry):
        rows = pl.ds(pl.multiple_of(i * 8, 8), 8)
        x, y, z = points[0, rows], points[1, rows], points[2, rows]
        force = [padded[3 + d, rows] for d in range(3)]
        t = 0
        power_x = jnp.ones_like(x)
        for a in range(DEGREE + 1):
            power_y = power_x
            for b in range(DEGREE + 1 - a):
                term = power_y
                for c in range(DEGREE + 1 - a - b):
                    for d in range(3):
                        v = term * force[d]
                        acc[d, t] += v[:, 0:128] + v[:, 128:256] + v[:, 256:384]
                    t += 1
                    if c < DEGREE - a - b:
                        term = term * z
                if b < DEGREE - a:
                    power_y = power_y * y
            if a < DEGREE:
                power_x = power_x * x
        return carry

    lax.fori_loop(0, cells // 8, moment_rows, 0)
    scale = 1.0 / math.sqrt(cells * n_cell * count)
    terms = acc.shape[1]
    sub = lax.broadcasted_iota(jnp.int32, (8, terms), 0)
    moments = jnp.zeros((8, terms), f32)
    for d in range(3):
        part = jnp.sum(acc[d], axis=1)
        row = lax.dot_general(jnp.ones((8, 128), f32), part, NT_DIMS, precision=highest, preferred_element_type=f32)
        moments = jnp.where(sub == d, row * scale, moments)
    mom_out[...] = jnp.zeros_like(mom_out)
    mom_out[:, 0:terms] = moments
    send(3, mom_out, mom_in)

    every(0, got_meta).wait_recv()
    whole = got_meta[0]
    for q in range(1, n_cell):
        whole = whole + got_meta[q]
    merged[...] = whole[0:1]
    meta[...] = whole[0:1]
    fetch = pltpu.make_async_copy(merged, meta_here, here_sems.at[0])
    fetch.start()
    fetch.wait()
    for q in range(n_cell):
        for k in range(2):
            send_b[q, k] = sent[meta_here[0, 4 * q + k]]
    send(2, send_b, got_b)
    got_b[me] = send_b[me]

    mom_in[me] = mom_out[...]
    every(3, mom_in).wait_recv()
    gathered = mom_in[0]
    for q in range(1, n_cell):
        gathered = gathered + mom_in[q]
    total[...] = gathered

    def side_copy(which, to):
        return pltpu.make_async_remote_copy(
            src_ref=total,
            dst_ref=beside.at[which],
            send_sem=side_send.at[which],
            recv_sem=side_recv.at[which],
            device_id={"slab": to},
            device_id_type=MESH,
        )

    up_copy, down_copy = side_copy(0, above), side_copy(1, below)
    up_copy.start()
    down_copy.start()
    up_copy.wait()
    down_copy.wait()
    lower = jnp.where(slab == 0, 0.0, beside[0])
    upper = jnp.where(slab == n_slab - 1, 0.0, beside[1])
    coef = jnp.zeros((8, NT), f32)
    loads[3].wait()
    for k, source in enumerate((total[...], lower, upper)):
        coef = coef + lax.dot_general(
            source[:, 0:NT], translate[k], NT_DIMS, precision=highest, preferred_element_type=f32
        )
    local[...] = coef[0:3]

    every(1, got_a).wait_recv()
    every(2, got_b).wait_recv()
    every(0, got_meta).wait_send()
    every(1, got_a).wait_send()
    every(2, got_b).wait_send()
    every(3, mom_in).wait_send()


def field_kernel(
    meta, owner, live, local, block, got, points, upsample_hbm,
    out,
    cell_list, source_list, upsample, packed, spread, up_high, up_low, left, right, table, columns, load_sem,
):
    load = pltpu.make_async_copy(upsample_hbm, upsample, load_sem)
    load.start()
    cells, count, up_count = out.shape[1], out.shape[2], upsample.shape[1]
    n_cell = owner.shape[2]

    def far_rows(i, carry):
        rows = pl.ds(pl.multiple_of(i * 16, 16), 16)
        x, y, z = points[0, rows], points[1, rows], points[2, rows]
        index = {}
        t = 0
        for a in range(DEGREE + 1):
            for b in range(DEGREE + 1 - a):
                for c in range(DEGREE + 1 - a - b):
                    index[a, b, c] = t
                    t += 1
        for d in range(3):
            in_x = None
            for a in range(DEGREE, -1, -1):
                in_y = None
                for b in range(DEGREE - a, -1, -1):
                    in_z = None
                    for c in range(DEGREE - a - b, -1, -1):
                        value = local[d, index[a, b, c]]
                        in_z = value if in_z is None else in_z * z + value
                    in_y = in_z if in_y is None else in_y * y + in_z
                in_x = in_y if in_x is None else in_x * x + in_y
            out[d, rows, :] = in_x[:, 0:count]
        return carry

    lax.fori_loop(0, cells // 16, far_rows, 0)

    row8 = lax.broadcasted_iota(jnp.int32, (8, 128), 0)
    lane8 = lax.broadcasted_iota(jnp.int32, (8, 128), 1)

    def take(n, data):
        last = jnp.zeros((8, 128), f32)
        for k in range(2):
            first, second = data[3 + 4 * k : 4 + 4 * k, 0:128], data[3 + 4 * k : 4 + 4 * k, 128:256]
            last = jnp.where(row8 == 4 * k, first, last)
            last = jnp.where(row8 == 4 * k + 1, pltpu.roll(first, 64, 1), last)
            last = jnp.where(row8 == 4 * k + 2, second, last)
        for d in range(3):
            at_centre = (row8 == d) & (lane8 == count - 256)
            last = jnp.where(at_centre, data[3:4, 192 + d : 193 + d], last)
        packed[n, :, 0:256] = data
        packed[n, :, 256:384] = last

    def clear(n, carry):
        cell_list[n] = 0
        source_list[n] = 0
        return carry

    lax.fori_loop(0, cells, clear, 0)

    def list_slot(q, n):
        for k in range(2):
            cell_list[n] = owner[0, k, q]
            source_list[n] = 2 * n_cell + 2 * q + k
            n = n + live[0, k, q]
            cell_list[n] = meta[0, 4 * q + k]
            source_list[n] = 2 * q + k
            n = n + meta[0, 4 * q + 2 + k]
        return n

    units = lax.fori_loop(0, n_cell, list_slot, jnp.int32(0))
    load.wait()

    up_high[...] = jnp.zeros_like(up_high)
    up_low[...] = jnp.zeros_like(up_low)
    whole = upsample[...]
    high = whole.astype(bf16)
    up_high[:, 0:up_count] = high
    up_low[:, 0:up_count] = (whole - high.astype(f32)).astype(bf16)

    def spread_units(i, carry):
        rows = pl.ds(i * 16, 16)
        for k in range(16):
            take(i * 16 + k, got[source_list[i * 16 + k]])
        data = packed[rows].reshape(128, LANES)[:, 0:count]
        first = data.astype(bf16)
        second = (data - first.astype(f32)).astype(bf16)
        result = (
            jnp.dot(first, up_high[...], preferred_element_type=f32)
            + jnp.dot(second, up_high[...], preferred_element_type=f32)
            + jnp.dot(first, up_low[...], preferred_element_type=f32)
        )
        spread[rows] = result.reshape(16, 8, UP_LANES)
        return carry

    lax.fori_loop(0, (units + 15) // 16, spread_units, 0)

    def build(u):
        cell = cell_list[u]
        target = block[cell]
        row = lax.broadcasted_iota(jnp.int32, (8, UP_LANES), 0)
        between = packed[u][:, count : count + 1] - target[:, count : count + 1]
        z = jnp.where(row < 3, STRETCH * (spread[u] + between), spread[u])
        table[u] = z
        square = jnp.sum(jnp.where(row < 3, z * z, 0.0), axis=0, keepdims=True) + 1.0
        aligned = jnp.concatenate([z[4:8], z[0:4]], axis=0)
        product = jnp.sum(jnp.where(row < 3, z * aligned, 0.0), axis=0, keepdims=True)
        feature = jnp.where(row < 3, -2.0 * z, jnp.where(row == 3, square, jnp.where(row == 7, -product, z)))
        f1, f2, f3 = split3(feature)
        constant = jnp.where(row < 3, 1.0, 0.0)
        for k, pair in enumerate(((f1, f2), (f1, f3), (f2, f1), (constant, jnp.zeros_like(constant)))):
            right[u, 16 * k : 16 * k + 16] = jnp.concatenate(pair, axis=0).astype(bf16)

        small = lax.broadcasted_iota(jnp.int32, (8, LANES), 0)
        y = jnp.where(small < 3, STRETCH * target, 0.0)
        yy = jnp.sum(y * y, axis=0, keepdims=True)
        y1, y2, y3 = split3(y)
        s1, s2, s3 = split3(yy)
        one = jnp.where(small == 3, 1.0, y1)
        squares = jnp.where(small == 0, s1, jnp.where(small == 1, s2, jnp.where(small == 2, s3, 0.0)))
        zero = jnp.zeros_like(y)
        order = [one, one, y2, one, y2, y3]
        lower = [jnp.concatenate([v[4:8], v[0:4]], axis=0) for v in order]
        for k, rows in enumerate((order + [squares, zero], lower + [zero, zero])):
            turned = jnp.transpose(jnp.concatenate(rows, axis=0))
            left[u, k] = turned[0:count].astype(bf16)

    def build_two(i, carry):
        build(2 * i)
        build(2 * i + 1)
        return carry

    lax.fori_loop(0, (units + 1) // 2, build_two, 0)

    columns[...] = jnp.zeros_like(columns)
    step = 40

    def finish(u):
        cell = cell_list[u]
        sums = jnp.transpose(columns[...])[0:8]
        small = lax.broadcasted_iota(jnp.int32, (8, LANES), 0)
        y = jnp.where(small < 3, STRETCH * block[cell], 0.0)
        velocity = (sums + y * sums[3:4]) * jnp.where(u < units, STRETCH / up_count, 0.0)
        for d in range(3):
            out[d, pl.ds(cell, 1), :] += velocity[d : d + 1, 0:count]

    def one_unit(u, carry):
        finish(jnp.maximum(u - 1, 0))
        for begin in range(0, count, step):
            size = min(step, count - begin)
            near = [jnp.zeros((size, 128), f32) for _ in range(4)]
            left_s = left[u, 0, begin : begin + size]
            left_p = left[u, 1, begin : begin + size]
            for c in range(UP_LANES // 128):
                lanes = slice(c * 128, c * 128 + 128)
                feature = right[u, :, lanes]
                inverse = lax.rsqrt(jnp.dot(left_s, feature, preferred_element_type=f32))
                projected = jnp.dot(left_p, feature, preferred_element_type=f32)
                cube = inverse * inverse * inverse
                along = inverse + cube
                across = cube * projected
                for d in range(3):
                    near[d] = near[d] - across * table[u, d : d + 1, lanes]
                    near[d] = near[d] + along * table[u, 4 + d : 5 + d, lanes]
                near[3] = near[3] + across
            for d in range(4):
                columns[begin : begin + size, d : d + 1] = jnp.sum(near[d], axis=1, keepdims=True)
        return carry

    def two_units(i, carry):
        one_unit(2 * i, 0)
        one_unit(2 * i + 1, 0)
        return carry

    lax.fori_loop(0, (units + 1) // 2, two_units, 0)
    finish(jnp.maximum((units + 1) // 2 * 2 - 1, 0))


def on_device(centers, offsets, forces, upsample, translate, owner_cell, peer_cell, live):
    cells, count = offsets.shape[1], offsets.shape[2]
    n_cell = owner_cell.shape[1]
    vmem = pl.BlockSpec(memory_space=pltpu.VMEM)
    smem = pl.BlockSpec(memory_space=pltpu.SMEM)
    hbm = pl.BlockSpec(memory_space=pltpu.HBM)
    slots = (n_cell, 2, 8, 256)
    owner, peer, live = (jnp.transpose(v, (0, 2, 1)) for v in (owner_cell, peer_cell, live))
    got, meta, block, points, local = pl.pallas_call(
        exchange_kernel,
        out_shape=(
            jax.ShapeDtypeStruct((2,) + slots, f32),
            jax.ShapeDtypeStruct((1, 128), jnp.int32),
            jax.ShapeDtypeStruct((cells, 8, LANES), f32),
            jax.ShapeDtypeStruct((3, cells, LANES), f32),
            jax.ShapeDtypeStruct((3, NT), f32),
        ),
        in_specs=[smem] * 3 + [hbm] * 4,
        out_specs=(vmem,) * 5,
        scratch_shapes=[
            pltpu.VMEM(centers.shape, f32),
            pltpu.VMEM(offsets.shape, f32),
            pltpu.VMEM(forces.shape, f32),
            pltpu.VMEM(translate.shape, f32),
            pltpu.VMEM((cells, 8, 256), f32),
            pltpu.VMEM(slots, f32),
            pltpu.VMEM(slots, f32),
            pltpu.VMEM((n_cell, 8, 128), jnp.int32),
            pltpu.VMEM((n_cell, 8, 128), jnp.int32),
            pltpu.VMEM((1, 128), jnp.int32),
            pltpu.SMEM((1, 128), jnp.int32),
            pltpu.VMEM((8, 256), f32),
            pltpu.VMEM((n_cell, 8, 256), f32),
            pltpu.VMEM((8, 256), f32),
            pltpu.VMEM((2, 8, 256), f32),
            pltpu.VMEM((6, cells, LANES), f32),
            pltpu.VMEM((3, 168, 8, 128), f32),
            pltpu.SemaphoreType.DMA((4,)),
            pltpu.SemaphoreType.DMA((4,)),
            pltpu.SemaphoreType.DMA((2,)),
            pltpu.SemaphoreType.DMA((2,)),
            pltpu.SemaphoreType.DMA((4,)),
        ],
        compiler_params=pltpu.CompilerParams(
            collective_id=0, has_side_effects=True, vmem_limit_bytes=60 * 1024 * 1024
        ),
        name="exchange",
    )(owner, peer, live, centers, offsets, forces, translate)
    return pl.pallas_call(
        field_kernel,
        out_shape=jax.ShapeDtypeStruct((3, cells, count), f32),
        in_specs=[smem] * 4 + [vmem] * 3 + [hbm],
        out_specs=vmem,
        scratch_shapes=[
            pltpu.SMEM((cells + 1,), jnp.int32),
            pltpu.SMEM((cells + 1,), jnp.int32),
            pltpu.VMEM(upsample.shape, f32),
            pltpu.VMEM((cells, 8, LANES), f32),
            pltpu.VMEM((cells, 8, UP_LANES), f32),
            pltpu.VMEM((count, UP_LANES), bf16),
            pltpu.VMEM((count, UP_LANES), bf16),
            pltpu.VMEM((cells, 2, count, 64), bf16),
            pltpu.VMEM((cells, 64, UP_LANES), bf16),
            pltpu.VMEM((cells, 8, UP_LANES), f32),
            pltpu.VMEM((LANES, 128), f32),
            pltpu.SemaphoreType.DMA,
        ],
        compiler_params=pltpu.CompilerParams(vmem_limit_bytes=61 * 1024 * 1024),
        name="field",
    )(meta, owner, live, local, block, got.reshape(4 * n_cell, 8, 256), points, upsample)


def solution(mesh):
    return jax.shard_map(
        on_device,
        mesh=mesh,
        in_specs=(
            P(None, ("slab", "cell")),
            P(None, ("slab", "cell"), None),
            P(None, ("slab", "cell"), None),
            P(),
            P(),
            P(("slab", "cell"), None, None),
            P(("slab", "cell"), None, None),
            P(("slab", "cell"), None, None),
        ),
        out_specs=P(None, ("slab", "cell"), None),
        check_vma=False,
    )
```
